128 devices in a mesh: dp: 4 (over z), seq: 32 (over x, y, core).
Axes of the slice: x: 4, y: 4, z: 4, core: 2. Of those that a mesh axis runs over, the one named last changes fastest.
Arguments:
- group_samples: bfloat16 [4, 32, 193, 2560], P('dp', 'seq'), may hold values from -6 to 6
- group_lengths: int32 [4, 32], P('dp', 'seq'), may hold values from 64 to 192, as said below
- group_offsets: int32 [4, 32], P('dp', 'seq'), may hold values from 0 to 4032, as said below
- conv_first: bfloat16 [80, 512], replicated, may hold values from -0.625 to 0.625
- conv_middle: bfloat16 [4, 1536, 512], replicated, may hold values from -0.15625 to 0.15625
- conv_last: bfloat16 [2, 1024, 512], replicated, may hold values from -0.1875 to 0.1875
- feat_gain: float32 [512], replicated, may hold values from 0.1 to 1.9
- proj_weight: bfloat16 [512, 1280], replicated, may hold values from -0.25 to 0.25
- proj_bias: float32 [1280], replicated, may hold values from -3 to 3
- attn_gain: float32 [1280], replicated, may hold values from 0.1 to 1.9
- attn_weight: bfloat16 [1280, 2560], P(None, ('dp', 'seq'))
Outputs:
- encoded: bfloat16 [4, 4096, 1280], P('dp', 'seq')
The draws below stay inside these ranges and needn't reach their ends.
Inputs may be any that keep to these rules, and one draw needn't show every extreme that they name: `group_lengths`: each group has 64 to 192 frames and in every night some group has exactly 192. Groups 2 k and 2 k + 1 of a night together have 2 * 128 frames. The last group of every night has 64 frames. `group_offsets`: groups lie in frame order, end to end: group 2 k starts at frame 2 k * 128 and group 2 k + 1 starts where group 2 k ends.
All inputs are finite; a program needn't handle non-finite values.
Results may differ from the reference program's by a relative error of at most 0.035.
Values may be sent and summed in bfloat16 or wider, within the bound.
A program may use at most 192 MiB of HBM per device.

```python
import jax
import jax.numpy as jnp
from jax import lax

CHANS = 8
CONV = 512
D = 1280
HEADS = 8
HD = 80
FR_DEV = 128
ROWS = 193
BLOCK = 2560
SEQ = 4096
NIGHTS = 4
GROUPS = 32


def group_plan(key):

    def one_night(night_key):
        first_key, second_key, third_key = jax.random.split(night_key, 3)
        half_len = FR_DEV // 2
        pair_count = GROUPS // 2
        pair_ids = jnp.arange(pair_count, dtype=jnp.int32)
        shifts = jax.random.randint(second_key, (pair_count,), 0, half_len + 1).astype(jnp.int32)
        full_pair = jax.random.randint(first_key, (), 0, pair_count).astype(jnp.int32)
        shifts = jnp.where(pair_ids == full_pair, half_len, shifts).astype(jnp.int32)
        shifts = jnp.where(pair_ids == pair_count - 1, half_len, shifts).astype(jnp.int32)
        signs = (2 * jax.random.randint(third_key, (pair_count,), 0, 2) - 1).astype(jnp.int32)
        signs = jnp.where(pair_ids == pair_count - 1, 1, signs).astype(jnp.int32)
        even_len = (FR_DEV + signs * shifts).astype(jnp.int32)
        odd_len = (2 * FR_DEV - even_len).astype(jnp.int32)
        lengths = jnp.stack([even_len, odd_len], axis=1).reshape(GROUPS).astype(jnp.int32)
        pair_start = (pair_ids * 2 * FR_DEV).astype(jnp.int32)
        offsets = jnp.stack([pair_start, pair_start + even_len], axis=1).reshape(GROUPS).astype(jnp.int32)
        return (lengths, offsets)
    night_keys = jax.random.split(jax.random.fold_in(key, 11), NIGHTS)
    return jax.vmap(one_night)(night_keys)


def draw_group_lengths(key, part):
    return group_plan(key)[0]


def draw_group_offsets(key, part):
    return group_plan(key)[1]


def draw_attn_weight(key, part):
    inner_width = HEADS * HD
    query_key, key_key, value_key, out_key = jax.random.split(jax.random.fold_in(key, 5), 4)
    keys_w = jax.random.normal(key_key, (D, inner_width), jnp.float32) * (2.0 / jnp.sqrt(jnp.float32(D)))
    own_queries = jax.random.normal(query_key, (D, inner_width), jnp.float32) * (2.0 / jnp.sqrt(jnp.float32(D)))
    queries_w = own_queries
    values_w = jax.random.normal(value_key, (D, inner_width), jnp.float32) / jnp.sqrt(jnp.float32(D))
    out_w = jax.random.normal(out_key, (D, inner_width), jnp.float32) / jnp.sqrt(jnp.float32(inner_width))
    return jnp.concatenate([queries_w, keys_w, values_w, out_w], axis=1).astype(jnp.bfloat16)


def block_scale(own_key, dims, cuts, least, largest):
    factor_of, own = 1.0, jax.random.fold_in(own_key, 6)
    for dim, parts in cuts:
        heights = jnp.exp(jax.random.uniform(jax.random.fold_in(own, dim), (parts,), jnp.float32, least / len(cuts), largest / len(cuts)))
        factor_of = factor_of * jnp.repeat(heights, dims[dim] // parts).reshape([-1 if axis == dim else 1 for axis in range(len(dims))])
    return factor_of


def bell_draw(own_key, shape, width, most, cuts=(), kind=jnp.bfloat16):
    entries = width * jax.random.normal(own_key, shape, jnp.float32)
    if cuts:
        entries = entries * block_scale(own_key, shape, cuts, -0.22, 0.18)
    return jnp.clip(entries, -most, most).astype(kind)


def setup_inputs(seed: int = 0) -> dict:
    streams_of = jax.random.split(jax.random.key(seed), 12)
    return {
        "group_samples": bell_draw(streams_of[0], (NIGHTS, GROUPS, ROWS, BLOCK), 1.0, 6.0, ((0, 4), (1, 32))),
        "group_lengths": draw_group_lengths(jax.random.fold_in(streams_of[11], 71), 0),
        "group_offsets": draw_group_offsets(jax.random.fold_in(streams_of[11], 71), 0),
        "conv_first": bell_draw(streams_of[3], (10 * CHANS, CONV), (10 * CHANS) ** -0.5, 0.625),
        "conv_middle": bell_draw(streams_of[4], (4, 3 * CONV, CONV), (3 * CONV) ** -0.5, 0.15625),
        "conv_last": bell_draw(streams_of[5], (2, 2 * CONV, CONV), (2 * CONV) ** -0.5, 0.1875),
        "feat_gain": jnp.clip(1.0 + 0.18 * jax.random.normal(streams_of[6], (CONV,), jnp.float32), 0.1, 1.9),
        "proj_weight": bell_draw(streams_of[7], (CONV, D), CONV ** -0.5, 0.25),
        "proj_bias": bell_draw(streams_of[8], (D,), 0.5, 3.0, (), jnp.float32),
        "attn_gain": jnp.clip(1.0 + 0.18 * jax.random.normal(streams_of[9], (D,), jnp.float32), 0.1, 1.9),
        "attn_weight": draw_attn_weight(jax.random.fold_in(streams_of[11], 71), 0),
    }


def layer_norm(values):
    center = lax.optimization_barrier(jnp.mean(values, axis=-1, keepdims=True))
    spread = lax.optimization_barrier(jnp.mean((values - center) ** 2, axis=-1, keepdims=True))
    return (values - center) * lax.rsqrt(spread + 1e-05)

def settle(summed):
    return jax.nn.gelu(layer_norm(summed), approximate=False).astype(jnp.bfloat16)

def strided(activity, weight, kernel):
    frame_count, steps, chan_width = activity.shape
    out_len = (steps - kernel) // 2 + 1
    summed = jnp.zeros((frame_count * out_len, chan_width), jnp.float32)
    for tap_index in range(kernel):
        strided_part = activity[:, tap_index:tap_index + 2 * (out_len - 1) + 1:2].reshape(-1, chan_width)
        summed = summed + jnp.dot(strided_part, weight[tap_index * chan_width:(tap_index + 1) * chan_width], preferred_element_type=jnp.float32)
    return settle(summed).reshape(frame_count, out_len, chan_width)

def conv_stack(windows, conv_first, conv_middle, conv_last):
    frame_count = windows.shape[0]
    tap_block = conv_first.shape[0] // 2
    chan_width = conv_first.shape[1]
    sample_grid = windows.reshape(frame_count, windows.shape[1] // tap_block, tap_block)
    tap_pairs = jnp.concatenate([sample_grid[:, :-1], sample_grid[:, 1:]], axis=2)
    summed = jnp.dot(tap_pairs.reshape(-1, 2 * tap_block), conv_first, preferred_element_type=jnp.float32)
    activity = settle(summed).reshape(frame_count, -1, chan_width)
    for layer_index in range(conv_middle.shape[0]):
        activity = strided(activity, conv_middle[layer_index], 3)
    for layer_index in range(conv_last.shape[0]):
        activity = strided(activity, conv_last[layer_index], 2)
    return activity.reshape(frame_count, chan_width)

def night_windows(samples_night, lengths_night, offsets_night):
    frame_ids = jnp.arange(SEQ, dtype=jnp.int32)
    inside = (frame_ids[:, None] >= offsets_night[None, :]) & (frame_ids[:, None] < offsets_night[None, :] + lengths_night[None, :])
    owner = lax.optimization_barrier(jnp.sum(jnp.where(inside, jnp.arange(GROUPS, dtype=jnp.int32)[None, :], 0), axis=1)).astype(jnp.int32)
    local_ids = (frame_ids - offsets_night[owner]).astype(jnp.int32)
    head_rows = samples_night[owner, local_ids]
    next_rows = samples_night[owner, local_ids + 1][:, :BLOCK // 4]
    return jnp.concatenate([head_rows, next_rows], axis=1)

def attend_block(query_block, keys3, values3):
    scores = jnp.einsum('qhd,khd->hqk', query_block.astype(jnp.float32), keys3.astype(jnp.float32)) / jnp.sqrt(jnp.float32(HD))
    peak = lax.optimization_barrier(jnp.max(scores, axis=-1, keepdims=True))
    expo = jnp.exp(scores - peak)
    total = lax.optimization_barrier(jnp.sum(expo, axis=-1))
    weights = lax.optimization_barrier(expo.astype(jnp.bfloat16)).astype(jnp.float32)
    mixed = jnp.einsum('hqk,khd->qhd', weights, values3.astype(jnp.float32)) / jnp.transpose(total)[:, :, None]
    return mixed.reshape(query_block.shape[0], HEADS * HD).astype(jnp.bfloat16)

def reference(group_samples, group_lengths, group_offsets, conv_first, conv_middle, conv_last, feat_gain, proj_weight, proj_bias, attn_gain, attn_weight):
    inner_width = HEADS * HD
    results = []
    for night_index in range(NIGHTS):
        windows = night_windows(group_samples[night_index], group_lengths[night_index], group_offsets[night_index])
        blocks = windows.reshape(SEQ // FR_DEV, FR_DEV, windows.shape[1])
        frame_feat = lax.map(lambda blk: conv_stack(blk, conv_first, conv_middle, conv_last), blocks).reshape(SEQ, -1)
        normed_feat = (layer_norm(frame_feat.astype(jnp.float32)) * feat_gain).astype(jnp.bfloat16)
        hidden_x = (jnp.dot(normed_feat, proj_weight, preferred_element_type=jnp.float32) + proj_bias).astype(jnp.bfloat16)
        normed_x = (layer_norm(hidden_x.astype(jnp.float32)) * attn_gain).astype(jnp.bfloat16)
        projected = jnp.dot(normed_x, attn_weight[:, :3 * inner_width], preferred_element_type=jnp.float32).astype(jnp.bfloat16)
        queries = projected[:, :inner_width].reshape(SEQ, HEADS, HD)
        keys3 = projected[:, inner_width:2 * inner_width].reshape(SEQ, HEADS, HD)
        values3 = projected[:, 2 * inner_width:].reshape(SEQ, HEADS, HD)
        query_blocks = queries.reshape(SEQ // FR_DEV, FR_DEV, HEADS, HD)
        mixed = lax.map(lambda blk: attend_block(blk, keys3, values3), query_blocks).reshape(SEQ, inner_width)
        out_proj = lax.dot_general(mixed, attn_weight[:, 3 * inner_width:], (((1,), (1,)), ((), ())), preferred_element_type=jnp.float32)
        results.append((hidden_x.astype(jnp.float32) + out_proj).astype(jnp.bfloat16))
    return jnp.stack(results, axis=0)
```

```python
import functools

import jax
import jax.numpy as jnp
from jax import lax
from jax.experimental import pallas as pl
from jax.experimental.pallas import tpu as pltpu
from jax.sharding import PartitionSpec as P

HEADS = 8
FR = 128
CH = 512
TAIL = 16
SWAP = 80
BF = jnp.bfloat16
F32 = jnp.float32


def dot(a, b):
    return jnp.dot(a, b, preferred_element_type=F32)


def row_norm(v, eps):
    center = jnp.mean(v, axis=-1, keepdims=True)
    d = v - center
    spread = jnp.mean(d * d, axis=-1, keepdims=True)
    return d * lax.rsqrt(spread + eps)


def settle(acc, rows, eps, out):
    for r in range(0, rows, 64):
        n = min(64, rows - r)
        v = acc[r : r + n, :]
        center = jnp.mean(v, axis=-1, keepdims=True)
        d = v - center
        spread = jnp.mean(d * d, axis=-1, keepdims=True)
        u = d * lax.rsqrt(2.0 * spread + 2.0 * eps)
        out(r, n, (u + u * lax.erf(u)).astype(BF))


def conv_kernel(
    meta, own, arr, first, middle_hbm, last_hbm, gain, proj_hbm, bias, attn_gain,
    hidden_ref, normed_ref,
    x, a1, a2, a3, a4, a5, a6, t1, t2, t3, t4, acc0, acc1, middle, last, proj, sems,
):
    copies = [
        pltpu.make_async_copy(middle_hbm.at[l], middle.at[l], sems.at[l]) for l in range(4)
    ]
    copies.append(pltpu.make_async_copy(last_hbm, last, sems.at[4]))
    copies.append(pltpu.make_async_copy(proj_hbm, proj, sems.at[5]))
    for copy in copies:
        copy.start()

    is_odd = meta[0]
    even_len = meta[1]
    n1 = jnp.where(is_odd == 1, jnp.maximum(even_len - FR, 0), jnp.minimum(even_len, FR))
    own_rows = own.shape[0]

    def source(r):
        even = jnp.where(r < even_len, r, own_rows + r - even_len)
        odd = jnp.where(
            r + FR < even_len, own_rows + r + FR - (own_rows - SWAP), r + FR - even_len
        )
        return jnp.where(is_odd == 1, odd, even)

    def frame_of(shape):
        r = lax.broadcasted_iota(jnp.int32, shape, 0)
        return r

    def picks(width, base, step):
        r = lax.broadcasted_iota(jnp.int32, (FR + TAIL, width), 0)
        col = lax.broadcasted_iota(jnp.int32, (FR + TAIL, width), 1) + base
        src = jnp.where(
            r < FR, source(r) + step, source(jnp.where(r == FR, n1 - 1, FR - 1)) + 1
        )
        return (src == col).astype(F32).astype(BF)

    pick_own, pick_arr = picks(own_rows, 0, 0), picks(SWAP, own_rows, 0)
    for c in range(0, 2560, 512):
        x[:, c : c + 512] = (
            dot(pick_own, own[:, c : c + 512]) + dot(pick_arr, arr[:, c : c + 512])
        ).astype(BF)
    x[:, 2560:2688] = (
        dot(picks(own_rows, 0, 1), own[:, :128]) + dot(picks(SWAP, own_rows, 1), arr[:, :128])
    ).astype(BF)

    nr = lax.broadcasted_iota(jnp.int32, (FR, FR + TAIL), 0)
    nc = lax.broadcasted_iota(jnp.int32, (FR, FR + TAIL), 1)
    following = jnp.where(nr == n1 - 1, FR, jnp.where(nr == FR - 1, FR + 1, nr + 1))
    pick_next = (following == nc).astype(F32).astype(BF)

    def close(a, t):
        body = jnp.concatenate([a[0, :, :CH], t[0, :, :CH]], axis=0)
        a[a.shape[0] - 1, :, :CH] = dot(pick_next, body).astype(BF)

    def layer_one(u, acc, parity, half):
        offset = lax.rem(40 * u, 128)
        base = pl.multiple_of(40 * u - offset, 128)
        er = lax.broadcasted_iota(jnp.int32, (256, 80), 0)
        ec = lax.broadcasted_iota(jnp.int32, (256, 80), 1)
        weight = dot((er == ec + offset).astype(F32).astype(BF), first[...]).astype(BF)
        parts = [x[:FR, pl.ds(pl.multiple_of(base + 640 * b, 128), 256)] for b in range(4)]
        parts.append(x[FR:, pl.ds(base, 256)])
        acc[...] = dot(jnp.concatenate(parts, axis=0), weight)

        def out(r, n, val):
            if r < 4 * FR:
                a1[8 * (r // FR) + half, r % FR : r % FR + n, parity * CH : parity * CH + CH] = val
            else:
                t1[half, :, parity * CH : parity * CH + CH] = val

        settle(acc, 4 * FR + TAIL, 1e-5, out)

    def one_step(i, carry):
        layer_one(2 * i, acc0, 0, i)
        layer_one(2 * i + 1, acc1, 1, i)
        return carry

    lax.fori_loop(0, 8, one_step, 0)
    close(a1, t1)

    def three_taps(ain, start, count, rows, layer, acc):
        pairs = ain[pl.ds(start, count)].reshape(count * rows, 2 * CH)
        ahead = ain[pl.ds(start + 1, count), :, :CH].reshape(count * rows, CH)
        acc[: count * rows, :] = dot(
            jnp.concatenate([pairs, ahead], axis=1), middle[layer]
        )

    def main_chunk(ain, aout, layer, i, acc):
        three_taps(ain, 4 * i, 4, FR, layer, acc)

        def out(r, n, val):
            s = r // FR
            aout[2 * i + s // 2, r % FR : r % FR + n, (s % 2) * CH : (s % 2) * CH + CH] = val

        settle(acc, 4 * FR, 2e-5, out)

    def tail_chunk(tin, tout, layer, count, acc):
        three_taps(tin, 0, count, TAIL, layer, acc)

        def out(r, n, val):
            for k in range(n // TAIL):
                s = (r + k * TAIL) // TAIL
                tout[s // 2, :, (s % 2) * CH : (s % 2) * CH + CH] = val[k * TAIL : (k + 1) * TAIL]

        settle(acc, count * TAIL, 2e-5, out)

    def layer(ain, aout, tin, tout, index, chunks, tail_count):
        copies[index].wait()

        def step(i, carry):
            main_chunk(ain, aout, index, 2 * i, acc0)
            main_chunk(ain, aout, index, 2 * i + 1, acc1)
            return carry

        if chunks > 1:
            lax.fori_loop(0, chunks // 2, step, 0)
        else:
            main_chunk(ain, aout, index, 0, acc0)
        if tail_count:
            tail_chunk(tin, tout, index, tail_count, acc1)
            close(aout, tout)

    layer(a1, a2, t1, t2, 0, 8, 7)
    layer(a2, a3, t2, t3, 1, 4, 3)
    layer(a3, a4, t3, t4, 2, 2, 1)
    layer(a4, a5, None, None, 3, 1, 0)

    copies[4].wait()
    acc0[: 2 * FR, :] = dot(a5[...].reshape(2 * FR, 2 * CH), last[0])

    def out6(r, n, val):
        a6[r % FR : r % FR + n, (r // FR) * CH : (r // FR) * CH + CH] = val

    settle(acc0, 2 * FR, 2e-5, out6)
    acc1[:FR, :] = dot(a6[...], last[1])
    feats = []
    settle(acc1, FR, 2e-5, lambda r, n, val: feats.append(val))
    frame_feat = jnp.concatenate(feats, axis=0).astype(F32)
    normed_feat = (row_norm(frame_feat, 2e-5) * gain[...]).astype(BF)
    copies[5].wait()
    hidden = (dot(normed_feat, proj[...]) + bias[...]).astype(BF)
    hidden_ref[...] = hidden
    normed_ref[...] = (row_norm(hidden.astype(F32), 1e-5) * attn_gain[...]).astype(BF)


def conv_call(meta, own, arr, first, middle, last, gain, proj, bias, attn_gain):
    vmem = pl.BlockSpec(memory_space=pltpu.VMEM)
    hbm = pl.BlockSpec(memory_space=pl.ANY)
    width = proj.shape[1]
    return pl.pallas_call(
        conv_kernel,
        out_shape=[jax.ShapeDtypeStruct((FR, width), BF)] * 2,
        in_specs=[
            pl.BlockSpec(memory_space=pltpu.SMEM), vmem, vmem, vmem, hbm, hbm, vmem, hbm, vmem, vmem,
        ],
        out_specs=[vmem] * 2,
        scratch_shapes=[
            pltpu.VMEM((FR + TAIL, 2688), BF),
            pltpu.VMEM((33, FR, 2 * CH), BF),
            pltpu.VMEM((17, FR, 2 * CH), BF),
            pltpu.VMEM((9, FR, 2 * CH), BF),
            pltpu.VMEM((5, FR, 2 * CH), BF),
            pltpu.VMEM((2, FR, 2 * CH), BF),
            pltpu.VMEM((FR, 2 * CH), BF),
            pltpu.VMEM((8, TAIL, 2 * CH), BF),
            pltpu.VMEM((4, TAIL, 2 * CH), BF),
            pltpu.VMEM((2, TAIL, 2 * CH), BF),
            pltpu.VMEM((1, TAIL, 2 * CH), BF),
            pltpu.VMEM((4 * FR + TAIL, CH), F32),
            pltpu.VMEM((4 * FR + TAIL, CH), F32),
            pltpu.VMEM(middle.shape, BF),
            pltpu.VMEM(last.shape, BF),
            pltpu.VMEM(proj.shape, BF),
            pltpu.SemaphoreType.DMA((6,)),
        ],
        compiler_params=pltpu.CompilerParams(vmem_limit_bytes=56 << 20),
        cost_estimate=pl.CostEstimate(
            flops=16 * 10**9, bytes_accessed=14 * 10**6, transcendentals=9 * 10**6
        ),
        name="conv_stack",
    )(
        meta, own, arr, first, middle, last, gain.reshape(1, -1), proj, bias.reshape(1, -1),
        attn_gain.reshape(1, -1),
    )


def partner(value, axis):
    pairs = [(source, source ^ 1) for source in range(lax.axis_size(axis))]
    return lax.ppermute(value, axis, pairs)


def body(
    group_samples, group_lengths, group_offsets, conv_first, conv_middle, conv_last,
    feat_gain, proj_weight, proj_bias, attn_gain, attn_weight,
):
    panels = lax.all_gather(attn_weight, ("dp", "seq"), axis=1, tiled=True)
    inner_width = panels.shape[1] // 4
    head_size = inner_width // HEADS
    is_odd = lax.axis_index("seq") % 2
    samples = group_samples[0, 0]
    rows = samples.shape[0]
    length = group_lengths[0, 0]
    even_len = jnp.where(is_odd == 1, 2 * FR - length, length)
    outgoing = jnp.where(is_odd == 1, samples[:SWAP], samples[rows - SWAP :])
    arrived = partner(outgoing, "seq")
    meta = jnp.stack([is_odd, even_len]).astype(jnp.int32)
    hidden_x, normed_x = conv_call(
        meta, samples, arrived, conv_first, conv_middle, conv_last, feat_gain, proj_weight,
        proj_bias, attn_gain,
    )
    projected = jnp.dot(
        normed_x, panels[:, : 3 * inner_width], preferred_element_type=F32
    ).astype(BF)
    queries = projected[:, :inner_width]
    keys_local = projected[:, inner_width : 2 * inner_width]
    values_local = projected[:, 2 * inner_width :]
    scale = 1.0 / jnp.sqrt(jnp.float32(head_size))
    queries3 = queries.reshape(FR, HEADS, head_size)
    key_piece = lax.all_gather(keys_local, "seq", axis=0, tiled=True).reshape(-1, HEADS, head_size)
    value_piece = lax.all_gather(values_local, "seq", axis=0, tiled=True).reshape(
        -1, HEADS, head_size
    )
    scores = (
        jnp.einsum("qhd,khd->hqk", queries3, key_piece, preferred_element_type=F32) * scale
    )
    peak = jnp.max(scores, axis=-1)
    expo = jnp.exp(scores - peak[:, :, None])
    total = jnp.sum(expo, axis=-1)
    accum = jnp.einsum("hqk,khd->hqd", expo.astype(BF), value_piece, preferred_element_type=F32)
    mixed = (
        jnp.transpose(accum / total[:, :, None], (1, 0, 2)).reshape(FR, inner_width).astype(BF)
    )
    out_proj = lax.dot_general(
        mixed, panels[:, 3 * inner_width :], (((1,), (1,)), ((), ())), preferred_element_type=F32
    )
    encoded = (hidden_x.astype(F32) + out_proj).astype(BF)
    return encoded.reshape(1, FR, -1)


def solution(mesh):
    in_specs = (
        P("dp", "seq", None, None), P("dp", "seq"), P("dp", "seq"),
        P(), P(), P(), P(), P(), P(), P(), P(None, ("dp", "seq")),
    )
    out_specs = P("dp", "seq", None)
    return jax.shard_map(body, mesh=mesh, in_specs=in_specs, out_specs=out_specs, check_vma=False)
```

```python
import math

import jax
import jax.numpy as jnp
from jax import lax
from jax.experimental import pallas as pl
from jax.experimental.pallas import tpu as pltpu
from jax.sharding import PartitionSpec as P

FR = 128
CH = 512
TAIL = 16
BF = jnp.bfloat16
F32 = jnp.float32
SCALE = math.log2(math.e) / math.sqrt(80)


def dot(a, b):
    return jnp.dot(a, b, preferred_element_type=F32)


def row_norm(v, eps):
    center = jnp.mean(v, axis=-1, keepdims=True)
    d = v - center
    spread = jnp.mean(d * d, axis=-1, keepdims=True)
    return d * lax.rsqrt(spread + eps)


def settle(acc, rows, eps, out):
    for r in range(0, rows, 64):
        n = min(64, rows - r)
        v = acc[r : r + n, :]
        center = jnp.mean(v, axis=-1, keepdims=True)
        d = v - center
        spread = jnp.mean(d * d, axis=-1, keepdims=True)
        u = d * lax.rsqrt(2.0 * spread + 2.0 * eps)
        out(r, n, (u + u * lax.erf(u)).astype(BF))


MESH = pl.DeviceIdType.MESH
NT = (((1,), (1,)), ((), ()))


def onehot(mask):
    return mask.astype(F32).astype(BF)


def kernel(
    length, samples_hbm, shard, first, middle_hbm, last_hbm, gain, proj_hbm, bias, attn_gain,
    out_ref,
    own, arr, x, a1, a2, a3, a4, a5, a6, t1, t2, t3, t4, acc0, acc1, middle, last, proj,
    zbuf, wblk, wbuf, normed2, hidden_buf, ysend, qkv, kvbuf, qs, peak, total, accum,
    mout, mbuf, part, psend, precv, sems, send_sems, recv_sems,
):
    me = lax.axis_index("seq")
    night = lax.axis_index("dp")
    core = me % 2
    chip = me // 2
    cx, cy = chip // 4, chip % 4
    ha = jnp.where(core == 0, cy, cx)
    qb = jnp.where(core == 0, cx, cy)
    half = cx // 2
    mate = me + 1 - 2 * core

    def place(a, b):
        return jnp.where(core == 0, (b * 4 + a) * 2, (a * 4 + b) * 2 + 1)

    def remote(src, dst, k, r, device):
        return pltpu.make_async_remote_copy(
            src_ref=src, dst_ref=dst, send_sem=send_sems.at[k], recv_sem=recv_sems.at[r],
            device_id=device, device_id_type=MESH,
        )

    barrier = pltpu.get_barrier_semaphore()

    def greet(device):
        pl.semaphore_signal(barrier, inc=1, device_id=device, device_id_type=MESH)

    greet({"seq": mate})
    for d in range(1, 4):
        greet({"dp": (night + d) % 4})
        greet({"seq": place((ha + d) % 4, qb)})
        greet({"seq": place(ha, (qb + d) % 4)})
    for k in range(16):
        source = 16 * core + k

        @pl.when(source != me)
        def _():
            greet({"seq": source})

    in_set = jnp.where(half == core, 1, 0)
    pl.semaphore_wait(barrier, 26 - in_set)

    swap = remote(samples_hbm, arr, 20, 20, {"seq": mate})
    swap.start()
    zcopies = [
        remote(shard, zbuf.at[night], 16 + d, 16 + (4 - d) % 4, {"dp": (night + d) % 4})
        for d in range(1, 4)
    ]
    for copy in zcopies:
        copy.start()
    own_copy = pltpu.make_async_copy(samples_hbm, own, sems.at[6])
    own_copy.start()
    zown = pltpu.make_async_copy(shard, zbuf.at[night], sems.at[7])
    zown.start()
    copies = [
        pltpu.make_async_copy(middle_hbm.at[l], middle.at[l], sems.at[l]) for l in range(4)
    ]
    copies.append(pltpu.make_async_copy(last_hbm, last, sems.at[4]))
    copies.append(pltpu.make_async_copy(proj_hbm, proj, sems.at[5]))
    for copy in copies:
        copy.start()

    is_odd = core
    group_len = length[0, 0]
    even_len = jnp.where(is_odd == 1, 2 * FR - group_len, group_len)
    n1 = jnp.where(is_odd == 1, jnp.maximum(even_len - FR, 0), jnp.minimum(even_len, FR))
    own_rows = own.shape[0]

    def source(r):
        even = jnp.where(r < even_len, r, own_rows + r - even_len)
        odd = jnp.where(
            r + FR < even_len, own_rows + r + FR, r + FR - even_len
        )
        return jnp.where(is_odd == 1, odd, even)

    def picks(width, base, step):
        r = lax.broadcasted_iota(jnp.int32, (FR + TAIL, width), 0)
        col = lax.broadcasted_iota(jnp.int32, (FR + TAIL, width), 1) + base
        src = jnp.where(
            r < FR, source(r) + step, source(jnp.where(r == FR, n1 - 1, FR - 1)) + 1
        )
        return onehot(src == col)

    own_copy.wait()
    zown.wait()
    for copy in zcopies:
        copy.wait_recv()
    cr = lax.broadcasted_iota(jnp.int32, (80, 128), 0)
    cc = lax.broadcasted_iota(jnp.int32, (80, 128), 1)
    wblk[...] = dot(
        onehot(cc == 32 * (cr // 20) + cr % 20), zbuf[...].reshape(128, zbuf.shape[2])
    ).astype(BF)
    slot = me - 16 * half

    def weight_copy(k):
        target = ((chip + k) % 16) * 2 + half
        return target, remote(wblk, wbuf.at[slot], k, slot, {"seq": target})

    for k in range(16):
        target, copy = weight_copy(k)

        @pl.when(target != me)
        def _():
            copy.start()

    @pl.when(half == core)
    def _():
        wbuf[slot] = wblk[...]

    swap.wait_recv()
    pick_own, pick_arr = picks(own_rows, 0, 0), picks(own_rows, own_rows, 0)
    for c in range(0, 2560, 512):
        x[:, c : c + 512] = (
            dot(pick_own, own[:, c : c + 512]) + dot(pick_arr, arr[:, c : c + 512])
        ).astype(BF)
    x[:, 2560:2688] = (
        dot(picks(own_rows, 0, 1), own[:, :128]) + dot(picks(own_rows, own_rows, 1), arr[:, :128])
    ).astype(BF)

    nr = lax.broadcasted_iota(jnp.int32, (FR, FR + TAIL), 0)
    nc = lax.broadcasted_iota(jnp.int32, (FR, FR + TAIL), 1)
    following = jnp.where(nr == n1 - 1, FR, jnp.where(nr == FR - 1, FR + 1, nr + 1))
    pick_next = (following == nc).astype(F32).astype(BF)

    def close(a, t):
        body = jnp.concatenate([a[0, :, :CH], t[0, :, :CH]], axis=0)
        a[a.shape[0] - 1, :, :CH] = dot(pick_next, body).astype(BF)

    def layer_one(u, acc, parity, half):
        offset = lax.rem(40 * u, 128)
        base = pl.multiple_of(40 * u - offset, 128)
        er = lax.broadcasted_iota(jnp.int32, (256, 80), 0)
        ec = lax.broadcasted_iota(jnp.int32, (256, 80), 1)
        weight = dot((er == ec + offset).astype(F32).astype(BF), first[...]).astype(BF)
        parts = [x[:FR, pl.ds(pl.multiple_of(base + 640 * b, 128), 256)] for b in range(4)]
        parts.append(x[FR:, pl.ds(base, 256)])
        acc[...] = dot(jnp.concatenate(parts, axis=0), weight)

        def out(r, n, val):
            if r < 4 * FR:
                a1[8 * (r // FR) + half, r % FR : r % FR + n, parity * CH : parity * CH + CH] = val
            else:
                t1[half, :, parity * CH : parity * CH + CH] = val

        settle(acc, 4 * FR + TAIL, 1e-5, out)

    def one_step(i, carry):
        layer_one(2 * i, acc0, 0, i)
        layer_one(2 * i + 1, acc1, 1, i)
        return carry

    lax.fori_loop(0, 8, one_step, 0)
    close(a1, t1)

    def three_taps(ain, start, count, rows, layer, acc):
        pairs = ain[pl.ds(start, count)].reshape(count * rows, 2 * CH)
        ahead = ain[pl.ds(start + 1, count), :, :CH].reshape(count * rows, CH)
        acc[: count * rows, :] = dot(
            jnp.concatenate([pairs, ahead], axis=1), middle[layer]
        )

    def main_chunk(ain, aout, layer, i, acc):
        three_taps(ain, 4 * i, 4, FR, layer, acc)

        def out(r, n, val):
            s = r // FR
            aout[2 * i + s // 2, r % FR : r % FR + n, (s % 2) * CH : (s % 2) * CH + CH] = val

        settle(acc, 4 * FR, 2e-5, out)

    def tail_chunk(tin, tout, layer, count, acc):
        three_taps(tin, 0, count, TAIL, layer, acc)

        def out(r, n, val):
            for k in range(n // TAIL):
                s = (r + k * TAIL) // TAIL
                tout[s // 2, :, (s % 2) * CH : (s % 2) * CH + CH] = val[k * TAIL : (k + 1) * TAIL]

        settle(acc, count * TAIL, 2e-5, out)

    def layer(ain, aout, tin, tout, index, chunks, tail_count):
        copies[index].wait()

        def step(i, carry):
            main_chunk(ain, aout, index, 2 * i, acc0)
            main_chunk(ain, aout, index, 2 * i + 1, acc1)
            return carry

        if chunks > 1:
            lax.fori_loop(0, chunks // 2, step, 0)
        else:
            main_chunk(ain, aout, index, 0, acc0)
        if tail_count:
            tail_chunk(tin, tout, index, tail_count, acc1)
            close(aout, tout)

    layer(a1, a2, t1, t2, 0, 8, 7)
    layer(a2, a3, t2, t3, 1, 4, 3)
    layer(a3, a4, t3, t4, 2, 2, 1)
    layer(a4, a5, None, None, 3, 1, 0)

    copies[4].wait()
    acc0[: 2 * FR, :] = dot(a5[...].reshape(2 * FR, 2 * CH), last[0])

    def out6(r, n, val):
        a6[r % FR : r % FR + n, (r // FR) * CH : (r // FR) * CH + CH] = val

    settle(acc0, 2 * FR, 2e-5, out6)
    acc1[:FR, :] = dot(a6[...], last[1])
    feats = []
    settle(acc1, FR, 2e-5, lambda r, n, val: feats.append(val))
    frame_feat = jnp.concatenate(feats, axis=0).astype(F32)
    normed_feat = (row_norm(frame_feat, 2e-5) * gain[...]).astype(BF)
    copies[5].wait()
    hidden = (dot(normed_feat, proj[...]) + bias[...]).astype(BF)
    hidden_buf[...] = hidden
    normed2[pl.ds(pl.multiple_of(core * FR, FR), FR), :] = (
        row_norm(hidden.astype(F32), 1e-5) * attn_gain[...]
    ).astype(BF)
    mine = normed2.at[pl.ds(pl.multiple_of(core * FR, FR), FR)]
    exchange = remote(mine, mine, 21, 21, {"seq": mate})
    exchange.start()
    for k in range(16):

        @pl.when(16 * core + k != me)
        def _():
            remote(wblk, wbuf.at[k], 0, k, {"seq": mate}).wait_recv()

    exchange.wait_recv()

    yr = lax.broadcasted_iota(jnp.int32, (320, 1), 0)
    row_scale = jnp.where(yr % 80 < 20, SCALE, 1.0).astype(F32)
    pr = lax.broadcasted_iota(jnp.int32, (240, 320), 0)
    pc = lax.broadcasted_iota(jnp.int32, (240, 320), 1)
    regroup = onehot(pc == 80 * ((pr % 80) // 20) + 20 * (pr // 80) + pr % 20)

    def project(h, carry):
        w = wbuf[pl.ds(4 * h, 4)].reshape(320, wbuf.shape[2])
        y = lax.dot_general(w, normed2[...], NT, preferred_element_type=F32)
        ysend[h] = dot(regroup, (y * row_scale).astype(BF)).astype(BF)
        return carry

    lax.fori_loop(0, 4, project, 0)

    heads = []
    for d in range(1, 4):
        to = (ha + d) % 4
        heads.append(
            remote(ysend.at[to], qkv.at[ha], 24 + d, 24 + (4 - d) % 4, {"seq": place(to, qb)})
        )
        heads[-1].start()
    keep = pltpu.make_async_copy(ysend.at[ha], qkv.at[ha], sems.at[8])
    keep.start()

    forwards = []

    def forward(d):
        src = qkv.at[(ha + d) % 4, pl.ds(80, 160)]
        for e in range(1, 4):
            copy = remote(
                src, kvbuf.at[qb, (ha + d) % 4], 28 + 4 * d + e, 28 + 4 * d + (4 - e) % 4,
                {"seq": place(ha, (qb + e) % 4)},
            )
            copy.start()
            forwards.append(copy)

    keep.wait()
    forward(0)
    for d in (3, 1, 2):
        remote(ysend.at[0], qkv.at[(ha + d) % 4], 24, 24 + d, {"seq": mate}).wait_recv()
        forward(d)

    mout[...] = jnp.zeros_like(mout)
    for i in range(4):
        qs[i] = jnp.transpose(qkv[i, :80, :].astype(F32)).astype(BF)

    def attend(keys, values, is_first):
        def step(i, carry):
            s = dot(qs[i], keys)
            top = jnp.max(s, axis=-1, keepdims=True)
            if not is_first:
                top = jnp.maximum(top, peak[i])
            p = jnp.exp2(s - top)
            mass = jnp.sum(p, axis=-1, keepdims=True)
            o = lax.dot_general(p.astype(BF), values, NT, preferred_element_type=F32)
            if not is_first:
                fade = jnp.exp2(peak[i] - top)
                mass = mass + total[i] * fade
                o = o + accum[i] * fade
            peak[i] = top
            total[i] = mass
            accum[i] = o
            return carry

        lax.fori_loop(0, 4, step, 0)

    attend(
        jnp.concatenate([qkv[i, 80:160, :] for i in range(4)], axis=1),
        jnp.concatenate([qkv[i, 160:240, :] for i in range(4)], axis=1),
        True,
    )
    for e in (1, 3, 2):
        b = (qb + e) % 4
        for d in range(4):
            remote(
                qkv.at[0, pl.ds(80, 160)], kvbuf.at[b, (ha + d) % 4], 28, 28 + 4 * d + e,
                {"seq": mate},
            ).wait_recv()
        attend(
            jnp.concatenate([kvbuf[b, i, :80, :] for i in range(4)], axis=1),
            jnp.concatenate([kvbuf[b, i, 80:, :] for i in range(4)], axis=1),
            False,
        )
    for i in range(4):
        mout[i, :, :80] = (accum[i] / total[i]).astype(BF)
    returns = []
    for d in range(1, 4):
        to = (ha + d) % 4
        returns.append(
            remote(mout.at[to], mbuf.at[ha], 44 + d, 44 + (4 - d) % 4, {"seq": place(to, qb)})
        )
        returns[-1].start()
    keep2 = pltpu.make_async_copy(mout.at[ha], mbuf.at[ha], sems.at[9])
    keep2.start()
    er = lax.broadcasted_iota(jnp.int32, (128, 320), 0)
    ec = lax.broadcasted_iota(jnp.int32, (128, 320), 1)
    spread = onehot((ec == 80 * (er // 20) + 60 + er % 20) & (er < 80))
    keep2.wait()
    for d in range(1, 4):
        remote(mout.at[0], mbuf.at[(ha + d) % 4], 44, 44 + d, {"seq": mate}).wait_recv()
    sums = None
    for h in range(4):
        wide = dot(mbuf[h], spread).astype(BF)
        term = dot(wide, wbuf[4 * h : 4 * h + 4].reshape(320, wbuf.shape[2]))
        sums = term if sums is None else sums + term
    part[...] = sums.reshape(2, FR, sums.shape[1])
    psend[...] = part[1 - core].astype(BF)
    last_swap = remote(psend, precv, 22, 22, {"seq": mate})
    last_swap.start()
    base = hidden_buf[...].astype(F32) + part[core]
    last_swap.wait_recv()
    out_ref[...] = (base + precv[...].astype(F32)).astype(BF)

    for copy in [swap, exchange, last_swap] + zcopies + heads + forwards + returns:
        copy.wait_send()
    for k in range(16):
        target, copy = weight_copy(k)

        @pl.when(target != me)
        def _():
            copy.wait_send()


def call(length, samples, shard, first, middle, last, gain, proj, bias, attn_gain):
    vmem = pl.BlockSpec(memory_space=pltpu.VMEM)
    hbm = pl.BlockSpec(memory_space=pl.ANY)
    rows, block = samples.shape
    width = proj.shape[1]
    return pl.pallas_call(
        kernel,
        out_shape=jax.ShapeDtypeStruct((FR, width), BF),
        in_specs=[
            pl.BlockSpec(memory_space=pltpu.SMEM), hbm, vmem, vmem, hbm, hbm, vmem, hbm, vmem, vmem,
        ],
        out_specs=vmem,
        scratch_shapes=[
            pltpu.VMEM((rows, block), BF),
            pltpu.VMEM((rows, block), BF),
            pltpu.VMEM((FR + TAIL, block + 128), BF),
            pltpu.VMEM((33, FR, 2 * CH), BF),
            pltpu.VMEM((17, FR, 2 * CH), BF),
            pltpu.VMEM((9, FR, 2 * CH), BF),
            pltpu.VMEM((5, FR, 2 * CH), BF),
            pltpu.VMEM((2, FR, 2 * CH), BF),
            pltpu.VMEM((FR, 2 * CH), BF),
            pltpu.VMEM((8, TAIL, 2 * CH), BF),
            pltpu.VMEM((4, TAIL, 2 * CH), BF),
            pltpu.VMEM((2, TAIL, 2 * CH), BF),
            pltpu.VMEM((1, TAIL, 2 * CH), BF),
            pltpu.VMEM((4 * FR + TAIL, CH), F32),
            pltpu.VMEM((4 * FR + TAIL, CH), F32),
            pltpu.VMEM(middle.shape, BF),
            pltpu.VMEM(last.shape, BF),
            pltpu.VMEM(proj.shape, BF),
            pltpu.VMEM((4, 32, width), BF),
            pltpu.VMEM((80, width), BF),
            pltpu.VMEM((16, 80, width), BF),
            pltpu.VMEM((2 * FR, width), BF),
            pltpu.VMEM((FR, width), BF),
            pltpu.VMEM((4, 240, 256), BF),
            pltpu.VMEM((4, 240, 256), BF),
            pltpu.VMEM((4, 4, 160, 256), BF),
            pltpu.VMEM((4, 256, 80), BF),
            pltpu.VMEM((4, 256, 1), F32),
            pltpu.VMEM((4, 256, 1), F32),
            pltpu.VMEM((4, 256, 80), F32),
            pltpu.VMEM((4, 256, 128), BF),
            pltpu.VMEM((4, 256, 128), BF),
            pltpu.VMEM((2, FR, width), F32),
            pltpu.VMEM((FR, width), BF),
            pltpu.VMEM((FR, width), BF),
            pltpu.SemaphoreType.DMA((10,)),
            pltpu.SemaphoreType.DMA((48,)),
            pltpu.SemaphoreType.DMA((48,)),
        ],
        compiler_params=pltpu.CompilerParams(
            vmem_limit_bytes=60 << 20, collective_id=0, has_side_effects=True
        ),
        cost_estimate=pl.CostEstimate(
            flops=20 * 10**9, bytes_accessed=20 * 10**6, transcendentals=13 * 10**6
        ),
        name="encoder",
    )(
        length, samples, shard, first, middle, last, gain.reshape(1, -1), proj,
        bias.reshape(1, -1), attn_gain.reshape(1, -1),
    )


def body(
    group_samples, group_lengths, group_offsets, conv_first, conv_middle, conv_last,
    feat_gain, proj_weight, proj_bias, attn_gain, attn_weight,
):
    shard = jnp.pad(attn_weight.T, ((0, 12), (0, 0)))
    encoded = call(
        group_lengths, group_samples[0, 0], shard, conv_first, conv_middle, conv_last,
        feat_gain, proj_weight, proj_bias, attn_gain,
    )
    return encoded.reshape(1, FR, -1)


def solution(mesh):
    in_specs = (
        P("dp", "seq", None, None), P("dp", "seq"), P("dp", "seq"),
        P(), P(), P(), P(), P(), P(), P(), P(None, ("dp", "seq")),
    )
    out_specs = P("dp", "seq", None)
    return jax.shard_map(body, mesh=mesh, in_specs=in_specs, out_specs=out_specs, check_vma=False)
```

```python
import math

import jax
import jax.numpy as jnp
from jax import lax
from jax.experimental import pallas as pl
from jax.experimental.pallas import tpu as pltpu
from jax.sharding import PartitionSpec as P

FR = 128
CH = 512
TAIL = 16
BF = jnp.bfloat16
F32 = jnp.float32
SCALE = math.log2(math.e) / math.sqrt(80)


def dot(a, b):
    return jnp.dot(a, b, preferred_element_type=F32)


def row_norm(v, eps):
    center = jnp.mean(v, axis=-1, keepdims=True)
    d = v - center
    spread = jnp.mean(d * d, axis=-1, keepdims=True)
    return d * lax.rsqrt(spread + eps)


def settle(acc, rows, eps, out):
    for r in range(0, rows, 64):
        n = min(64, rows - r)
        v = acc[r : r + n, :]
        center = jnp.mean(v, axis=-1, keepdims=True)
        d = v - center
        spread = jnp.mean(d * d, axis=-1, keepdims=True)
        u = d * lax.rsqrt(2.0 * spread + 2.0 * eps)
        out(r, n, (u + u * lax.erf(u)).astype(BF))


MESH = pl.DeviceIdType.MESH
NT = (((1,), (1,)), ((), ()))


def onehot(mask):
    return mask.astype(F32).astype(BF)


def kernel(
    length, samples_hbm, shard, first, middle_hbm, last_hbm, gain, proj_hbm, bias, attn_gain,
    out_ref,
    own, arr, x, a1, a2, a3, a4, a5, a6, t1, t2, t3, t4, acc0, acc1, middle, last, proj,
    zbuf, wblk, wbuf, normed2, hidden_buf, ysend, qkv, kvbuf, qs, peak, accum,
    mout, mbuf, part, psend, precv, sems, send_sems, recv_sems,
):
    me = lax.axis_index("seq")
    night = lax.axis_index("dp")
    core = me % 2
    chip = me // 2
    cx, cy = chip // 4, chip % 4
    ha = jnp.where(core == 0, cy, cx)
    qb = jnp.where(core == 0, cx, cy)
    half = cx // 2
    mate = me + 1 - 2 * core

    def place(a, b):
        return jnp.where(core == 0, (b * 4 + a) * 2, (a * 4 + b) * 2 + 1)

    def remote(src, dst, k, r, device):
        return pltpu.make_async_remote_copy(
            src_ref=src, dst_ref=dst, send_sem=send_sems.at[k], recv_sem=recv_sems.at[r],
            device_id=device, device_id_type=MESH,
        )

    barrier = pltpu.get_barrier_semaphore()

    def greet(device):
        pl.semaphore_signal(barrier, inc=1, device_id=device, device_id_type=MESH)

    def at(px, py, pc):
        return {"seq": (px * 4 + py) * 2 + pc}

    greet({"seq": mate})
    for d in range(1, 4):
        greet({"dp": (night + d) % 4})
        for pc in range(2):
            greet(at((cx + d) % 4, cy, pc))
            greet(at(cx, (cy + d) % 4, pc))
    pl.semaphore_wait(barrier, 16)

    swap = remote(samples_hbm, arr, 20, 20, {"seq": mate})
    swap.start()
    zcopies = [
        remote(shard, zbuf.at[night], 16 + d, 16 + (4 - d) % 4, {"dp": (night + d) % 4})
        for d in range(1, 4)
    ]
    for copy in zcopies:
        copy.start()
    own_copy = pltpu.make_async_copy(samples_hbm, own, sems.at[6])
    own_copy.start()
    zown = pltpu.make_async_copy(shard, zbuf.at[night], sems.at[7])
    zown.start()
    copies = [
        pltpu.make_async_copy(middle_hbm.at[l], middle.at[l], sems.at[l]) for l in range(4)
    ]
    copies.append(pltpu.make_async_copy(last_hbm, last, sems.at[4]))
    copies.append(pltpu.make_async_copy(proj_hbm, proj, sems.at[5]))
    for copy in copies:
        copy.start()

    is_odd = core
    group_len = length[0, 0]
    even_len = jnp.where(is_odd == 1, 2 * FR - group_len, group_len)
    n1 = jnp.where(is_odd == 1, jnp.maximum(even_len - FR, 0), jnp.minimum(even_len, FR))
    own_rows = own.shape[0]

    def source(r):
        even = jnp.where(r < even_len, r, own_rows + r - even_len)
        odd = jnp.where(
            r + FR < even_len, own_rows + r + FR, r + FR - even_len
        )
        return jnp.where(is_odd == 1, odd, even)

    def picks(width, base, step):
        r = lax.broadcasted_iota(jnp.int32, (FR + TAIL, width), 0)
        col = lax.broadcasted_iota(jnp.int32, (FR + TAIL, width), 1) + base
        src = jnp.where(
            r < FR, source(r) + step, source(jnp.where(r == FR, n1 - 1, FR - 1)) + 1
        )
        return onehot(src == col)

    own_copy.wait()
    zown.wait()
    for copy in zcopies:
        copy.wait_recv()
    cr = lax.broadcasted_iota(jnp.int32, (80, 20), 0)
    cc = lax.broadcasted_iota(jnp.int32, (80, 20), 1)
    packed = sum(dot(onehot(cr == cc + 20 * p), zbuf[p]) for p in range(4)).astype(BF)
    wide = packed.shape[1] // 2
    wblk[0] = packed[:, :wide]
    wblk[1] = packed[:, wide:]
    slot = me - 16 * half
    first_hops = []
    for d in range(4):
        ty, tx = (cy + d) % 4, (cx + d) % 4
        first_hops.append((
            at(cx, ty, half),
            remote(wblk.at[0], wbuf.at[0, slot], 48 + d, 48 + slot % 8, at(cx, ty, half)),
        ))
        first_hops.append((
            at(tx, cy, half),
            remote(
                wblk.at[1], wbuf.at[1, slot], 52 + d, 56 + (cx % 2) * 2 + core, at(tx, cy, half)
            ),
        ))
    for target, copy in first_hops:

        @pl.when(target["seq"] != me)
        def _():
            copy.start()

    @pl.when(half == core)
    def _():
        wbuf[0, slot] = wblk[0]
        wbuf[1, slot] = wblk[1]

    row_slots = pl.ds(8 * (cx % 2), 8)
    x_hops = [
        remote(
            wbuf.at[0, row_slots], wbuf.at[0, row_slots], 60 + d, 60 + cx % 2,
            at((cx + d) % 4, cy, core),
        )
        for d in range(1, 4)
    ]
    y_hops = [
        remote(
            wbuf.at[1, pl.ds(8 * p + 2 * cy, 2)], wbuf.at[1, pl.ds(8 * p + 2 * cy, 2)],
            64 + 2 * d + p, 64 + 2 * (4 - d) + p, at(cx, (cy + d) % 4, core),
        )
        for d in range(1, 4)
        for p in range(2)
    ]

    def second_hops():
        for k in range(8):

            @pl.when((half == core) & (k != slot % 8))
            def _():
                remote(
                    wblk.at[0], wbuf.at[0, 8 * (cx % 2) + k], 48, 48 + k, {"seq": mate}
                ).wait_recv()

        @pl.when(half == core)
        def _():
            for copy in x_hops:
                copy.start()

        for k in range(4):
            from_x, from_core = 2 * core + k // 2, k % 2

            @pl.when((from_x != cx) | (from_core != core))
            def _():
                remote(
                    wblk.at[1], wbuf.at[1, 8 * (k // 2) + 2 * cy + from_core], 52, 56 + k,
                    {"seq": mate},
                ).wait_recv()

        for copy in y_hops:
            copy.start()

    def weights_arrived():
        for p in range(2):

            @pl.when(2 * core + p != cx)
            def _():
                remote(
                    wbuf.at[0, pl.ds(8 * p, 8)], wbuf.at[0, pl.ds(8 * p, 8)], 60, 60 + p,
                    {"seq": mate},
                ).wait_recv()

        for d in range(1, 4):
            for p in range(2):
                block = wbuf.at[1, pl.ds(8 * p + 2 * ((cy + d) % 4), 2)]
                remote(block, block, 64, 64 + 2 * d + p, {"seq": mate}).wait_recv()

    def weights_sent():
        for target, copy in first_hops:

            @pl.when(target["seq"] != me)
            def _():
                copy.wait_send()

        @pl.when(half == core)
        def _():
            for copy in x_hops:
                copy.wait_send()

        for copy in y_hops:
            copy.wait_send()

    swap.wait_recv()
    pick_own, pick_arr = picks(own_rows, 0, 0), picks(own_rows, own_rows, 0)
    for c in range(0, 2560, 512):
        x[:, c : c + 512] = (
            dot(pick_own, own[:, c : c + 512]) + dot(pick_arr, arr[:, c : c + 512])
        ).astype(BF)
    x[:, 2560:2688] = (
        dot(picks(own_rows, 0, 1), own[:, :128]) + dot(picks(own_rows, own_rows, 1), arr[:, :128])
    ).astype(BF)

    nr = lax.broadcasted_iota(jnp.int32, (FR, FR + TAIL), 0)
    nc = lax.broadcasted_iota(jnp.int32, (FR, FR + TAIL), 1)
    following = jnp.where(nr == n1 - 1, FR, jnp.where(nr == FR - 1, FR + 1, nr + 1))
    pick_next = (following == nc).astype(F32).astype(BF)

    def close(a, t):
        body = jnp.concatenate([a[0, :, :CH], t[0, :, :CH]], axis=0)
        a[a.shape[0] - 1, :, :CH] = dot(pick_next, body).astype(BF)

    def layer_one(u, acc, parity, half):
        offset = lax.rem(40 * u, 128)
        base = pl.multiple_of(40 * u - offset, 128)
        er = lax.broadcasted_iota(jnp.int32, (256, 80), 0)
        ec = lax.broadcasted_iota(jnp.int32, (256, 80), 1)
        weight = dot((er == ec + offset).astype(F32).astype(BF), first[...]).astype(BF)
        parts = [x[:FR, pl.ds(pl.multiple_of(base + 640 * b, 128), 256)] for b in range(4)]
        parts.append(x[FR:, pl.ds(base, 256)])
        acc[...] = dot(jnp.concatenate(parts, axis=0), weight)

        def out(r, n, val):
            if r < 4 * FR:
                a1[8 * (r // FR) + half, r % FR : r % FR + n, parity * CH : parity * CH + CH] = val
            else:
                t1[half, :, parity * CH : parity * CH + CH] = val

        settle(acc, 4 * FR + TAIL, 1e-5, out)

    def one_step(i, carry):
        layer_one(2 * i, acc0, 0, i)
        layer_one(2 * i + 1, acc1, 1, i)
        return carry

    lax.fori_loop(0, 4, one_step, 0)
    second_hops()
    lax.fori_loop(4, 8, one_step, 0)
    close(a1, t1)

    def three_taps(ain, start, count, rows, layer, acc):
        pairs = ain[pl.ds(start, count)].reshape(count * rows, 2 * CH)
        ahead = ain[pl.ds(start + 1, count), :, :CH].reshape(count * rows, CH)
        acc[: count * rows, :] = dot(
            jnp.concatenate([pairs, ahead], axis=1), middle[layer]
        )

    def main_chunk(ain, aout, layer, i, acc):
        three_taps(ain, 4 * i, 4, FR, layer, acc)

        def out(r, n, val):
            s = r // FR
            aout[2 * i + s // 2, r % FR : r % FR + n, (s % 2) * CH : (s % 2) * CH + CH] = val

        settle(acc, 4 * FR, 2e-5, out)

    def tail_chunk(tin, tout, layer, count, acc):
        three_taps(tin, 0, count, TAIL, layer, acc)

        def out(r, n, val):
            for k in range(n // TAIL):
                s = (r + k * TAIL) // TAIL
                tout[s // 2, :, (s % 2) * CH : (s % 2) * CH + CH] = val[k * TAIL : (k + 1) * TAIL]

        settle(acc, count * TAIL, 2e-5, out)

    def layer(ain, aout, tin, tout, index, chunks, tail_count):
        copies[index].wait()

        def step(i, carry):
            main_chunk(ain, aout, index, 2 * i, acc0)
            main_chunk(ain, aout, index, 2 * i + 1, acc1)
            return carry

        if chunks > 1:
            lax.fori_loop(0, chunks // 2, step, 0)
        else:
            main_chunk(ain, aout, index, 0, acc0)
        if tail_count:
            tail_chunk(tin, tout, index, tail_count, acc1)
            close(aout, tout)

    layer(a1, a2, t1, t2, 0, 8, 7)
    layer(a2, a3, t2, t3, 1, 4, 3)
    layer(a3, a4, t3, t4, 2, 2, 1)
    layer(a4, a5, None, None, 3, 1, 0)

    copies[4].wait()
    acc0[: 2 * FR, :] = dot(a5[...].reshape(2 * FR, 2 * CH), last[0])

    def out6(r, n, val):
        a6[r % FR : r % FR + n, (r // FR) * CH : (r // FR) * CH + CH] = val

    settle(acc0, 2 * FR, 2e-5, out6)
    acc1[:FR, :] = dot(a6[...], last[1])
    feats = []
    settle(acc1, FR, 2e-5, lambda r, n, val: feats.append(val))
    frame_feat = jnp.concatenate(feats, axis=0).astype(F32)
    normed_feat = (row_norm(frame_feat, 2e-5) * gain[...]).astype(BF)
    copies[5].wait()
    hidden = (dot(normed_feat, proj[...]) + bias[...]).astype(BF)
    hidden_buf[...] = hidden
    normed2[pl.ds(pl.multiple_of(core * FR, FR), FR), :] = (
        row_norm(hidden.astype(F32), 1e-5) * attn_gain[...]
    ).astype(BF)
    mine = normed2.at[pl.ds(pl.multiple_of(core * FR, FR), FR)]
    exchange = remote(mine, mine, 21, 21, {"seq": mate})
    exchange.start()
    weights_arrived()
    exchange.wait_recv()

    def head_weights(h):
        return jnp.concatenate(
            [wbuf[p, pl.ds(4 * h, 4)].reshape(320, wbuf.shape[3]) for p in range(2)], axis=1
        )

    yr = lax.broadcasted_iota(jnp.int32, (320, 1), 0)
    row_scale = jnp.where(yr % 80 < 20, SCALE, 1.0).astype(F32)
    pr = lax.broadcasted_iota(jnp.int32, (240, 320), 0)
    pc = lax.broadcasted_iota(jnp.int32, (240, 320), 1)
    regroup = onehot(pc == 80 * ((pr % 80) // 20) + 20 * (pr // 80) + pr % 20)

    def project(h, carry):
        y = lax.dot_general(head_weights(h), normed2[...], NT, preferred_element_type=F32)
        ysend[h] = dot(regroup, (y * row_scale).astype(BF)).astype(BF)
        return carry

    lax.fori_loop(0, 4, project, 0)

    heads = []
    for d in range(1, 4):
        to = (ha + d) % 4
        heads.append(
            remote(ysend.at[to], qkv.at[ha], 24 + d, 24 + (4 - d) % 4, {"seq": place(to, qb)})
        )
        heads[-1].start()
    keep = pltpu.make_async_copy(ysend.at[ha], qkv.at[ha], sems.at[8])
    keep.start()

    forwards = []

    def forward(d):
        src = qkv.at[(ha + d) % 4, pl.ds(80, 160)]
        for e in range(1, 4):
            copy = remote(
                src, kvbuf.at[qb, (ha + d) % 4], 28 + 4 * d + e, 28 + 4 * d + (4 - e) % 4,
                {"seq": place(ha, (qb + e) % 4)},
            )
            copy.start()
            forwards.append(copy)

    keep.wait()
    forward(0)
    for d in (3, 1, 2):
        remote(ysend.at[0], qkv.at[(ha + d) % 4], 24, 24 + d, {"seq": mate}).wait_recv()
        forward(d)

    mout[...] = jnp.zeros_like(mout)
    for i in range(4):
        qs[i] = jnp.transpose(qkv[i, :80, :].astype(F32)).astype(BF)

    def masses(values):
        ones = jnp.ones((16, values.shape[1]), BF)
        return jnp.concatenate([values, ones], axis=0)

    def attend(keys, values, is_first):
        def step(i, carry):
            s = dot(qs[i], keys)
            top = jnp.max(s, axis=-1, keepdims=True)
            if not is_first:
                top = jnp.maximum(top, peak[i])
            p = jnp.exp2(s - top)
            o = lax.dot_general(p.astype(BF), masses(values), NT, preferred_element_type=F32)
            if not is_first:
                fade = jnp.exp2(peak[i] - top)
                o = o + accum[i] * fade
            peak[i] = top
            accum[i] = o
            return carry

        lax.fori_loop(0, 2, lambda i, c: step(2 * i + 1, step(2 * i, c)), 0)

    attend(
        jnp.concatenate([qkv[i, 80:160, :] for i in range(4)], axis=1),
        jnp.concatenate([qkv[i, 160:240, :] for i in range(4)], axis=1),
        True,
    )
    for e in (1, 3, 2):
        b = (qb + e) % 4
        for d in range(4):
            remote(
                qkv.at[0, pl.ds(80, 160)], kvbuf.at[b, (ha + d) % 4], 28, 28 + 4 * d + e,
                {"seq": mate},
            ).wait_recv()
        attend(
            jnp.concatenate([kvbuf[b, i, :80, :] for i in range(4)], axis=1),
            jnp.concatenate([kvbuf[b, i, 80:, :] for i in range(4)], axis=1),
            False,
        )
    for i in range(4):
        mout[i, :, :80] = (accum[i, :, :80] / accum[i, :, 80:81]).astype(BF)
    returns = []
    for d in range(1, 4):
        to = (ha + d) % 4
        returns.append(
            remote(mout.at[to], mbuf.at[ha], 44 + d, 44 + (4 - d) % 4, {"seq": place(to, qb)})
        )
        returns[-1].start()
    keep2 = pltpu.make_async_copy(mout.at[ha], mbuf.at[ha], sems.at[9])
    keep2.start()
    er = lax.broadcasted_iota(jnp.int32, (128, 320), 0)
    ec = lax.broadcasted_iota(jnp.int32, (128, 320), 1)
    spread = onehot((ec == 80 * (er // 20) + 60 + er % 20) & (er < 80))
    keep2.wait()
    for d in range(1, 4):
        remote(mout.at[0], mbuf.at[(ha + d) % 4], 44, 44 + d, {"seq": mate}).wait_recv()
    sums = None
    for h in range(4):
        wide = dot(mbuf[h], spread).astype(BF)
        term = dot(wide, head_weights(h))
        sums = term if sums is None else sums + term
    part[...] = sums.reshape(2, FR, sums.shape[1])
    psend[...] = part[1 - core].astype(BF)
    last_swap = remote(psend, precv, 22, 22, {"seq": mate})
    last_swap.start()
    base = hidden_buf[...].astype(F32) + part[core]
    last_swap.wait_recv()
    out_ref[...] = (base + precv[...].astype(F32)).astype(BF)

    for copy in [swap, exchange, last_swap] + zcopies + heads + forwards + returns:
        copy.wait_send()
    weights_sent()


def call(length, samples, shard, first, middle, last, gain, proj, bias, attn_gain):
    vmem = pl.BlockSpec(memory_space=pltpu.VMEM)
    hbm = pl.BlockSpec(memory_space=pl.ANY)
    rows, block = samples.shape
    width = proj.shape[1]
    return pl.pallas_call(
        kernel,
        out_shape=jax.ShapeDtypeStruct((FR, width), BF),
        in_specs=[
            pl.BlockSpec(memory_space=pltpu.SMEM), hbm, hbm, vmem, hbm, hbm, vmem, hbm, vmem, vmem,
        ],
        out_specs=vmem,
        scratch_shapes=[
            pltpu.VMEM((rows, block), BF),
            pltpu.VMEM((rows, block), BF),
            pltpu.VMEM((FR + TAIL, block + 128), BF),
            pltpu.VMEM((33, FR, 2 * CH), BF),
            pltpu.VMEM((17, FR, 2 * CH), BF),
            pltpu.VMEM((9, FR, 2 * CH), BF),
            pltpu.VMEM((5, FR, 2 * CH), BF),
            pltpu.VMEM((2, FR, 2 * CH), BF),
            pltpu.VMEM((FR, 2 * CH), BF),
            pltpu.VMEM((8, TAIL, 2 * CH), BF),
            pltpu.VMEM((4, TAIL, 2 * CH), BF),
            pltpu.VMEM((2, TAIL, 2 * CH), BF),
            pltpu.VMEM((1, TAIL, 2 * CH), BF),
            pltpu.VMEM((4 * FR + TAIL, CH), F32),
            pltpu.VMEM((4 * FR + TAIL, CH), F32),
            pltpu.VMEM(middle.shape, BF),
            pltpu.VMEM(last.shape, BF),
            pltpu.VMEM(proj.shape, BF),
            pltpu.VMEM((4, 20, width), BF),
            pltpu.VMEM((2, 80, width // 2), BF),
            pltpu.VMEM((2, 16, 80, width // 2), BF),
            pltpu.VMEM((2 * FR, width), BF),
            pltpu.VMEM((FR, width), BF),
            pltpu.VMEM((4, 240, 256), BF),
            pltpu.VMEM((4, 240, 256), BF),
            pltpu.VMEM((4, 4, 160, 256), BF),
            pltpu.VMEM((4, 256, 80), BF),
            pltpu.VMEM((4, 256, 1), F32),
            pltpu.VMEM((4, 256, 96), F32),
            pltpu.VMEM((4, 256, 128), BF),
            pltpu.VMEM((4, 256, 128), BF),
            pltpu.VMEM((2, FR, width), F32),
            pltpu.VMEM((FR, width), BF),
            pltpu.VMEM((FR, width), BF),
            pltpu.SemaphoreType.DMA((10,)),
            pltpu.SemaphoreType.DMA((72,)),
            pltpu.SemaphoreType.DMA((72,)),
        ],
        compiler_params=pltpu.CompilerParams(
            vmem_limit_bytes=60 << 20, collective_id=0, has_side_effects=True
        ),
        cost_estimate=pl.CostEstimate(
            flops=20 * 10**9, bytes_accessed=20 * 10**6, transcendentals=13 * 10**6
        ),
        name="encoder",
    )(
        length, samples, shard, first, middle, last, gain, proj, bias,
        attn_gain,
    )


def body(
    group_samples, group_lengths, group_offsets, conv_first, conv_middle, conv_last,
    feat_gain, proj_weight, proj_bias, attn_gain, attn_weight,
):
    encoded = call(
        group_lengths, group_samples[0, 0], attn_weight.T, conv_first, conv_middle, conv_last,
        feat_gain, proj_weight, proj_bias, attn_gain,
    )
    return encoded.reshape(1, FR, -1)


def solution(mesh):
    in_specs = (
        P("dp", "seq", None, None), P("dp", "seq"), P("dp", "seq"),
        P(), P(), P(), P(), P(), P(), P(), P(None, ("dp", "seq")),
    )
    out_specs = P("dp", "seq", None)
    return jax.shard_map(body, mesh=mesh, in_specs=in_specs, out_specs=out_specs, check_vma=False)
```

```python
import math

import jax
import jax.numpy as jnp
from jax import lax
from jax.experimental import pallas as pl
from jax.experimental.pallas import tpu as pltpu
from jax.sharding import PartitionSpec as P

FR = 128
CH = 512
TAIL = 16
BF = jnp.bfloat16
F32 = jnp.float32
SCALE = math.log2(math.e) / math.sqrt(80)


def dot(a, b):
    return jnp.dot(a, b, preferred_element_type=F32)


def row_norm(v, eps):
    center = jnp.mean(v, axis=-1, keepdims=True)
    d = v - center
    spread = jnp.mean(d * d, axis=-1, keepdims=True)
    return d * lax.rsqrt(spread + eps)


def settle(acc, rows, eps, out):
    for r in range(0, rows, 64):
        n = min(64, rows - r)
        v = acc[r : r + n, :]
        center = jnp.mean(v, axis=-1, keepdims=True)
        d = v - center
        spread = jnp.mean(d * d, axis=-1, keepdims=True)
        u = d * lax.rsqrt(2.0 * spread + 2.0 * eps)
        out(r, n, (u + u * lax.erf(u)).astype(BF))


MESH = pl.DeviceIdType.MESH
NT = (((1,), (1,)), ((), ()))


def onehot(mask):
    return mask.astype(F32).astype(BF)


def kernel(
    length, samples_hbm, shard, first, middle_hbm, last_hbm, gain, proj_hbm, bias, attn_gain,
    out_ref,
    own, arr, x, a1, a2, a3, a4, a5, a6, t1, t2, t3, t4, acc0, acc1, middle, last, proj,
    shard_buf, zbuf, wblk, wbuf, normed2, hidden_buf, ysend, qkv, kvbuf, qs, peak, accum,
    mout, mbuf, widen, psend, precv, sems, send_sems, recv_sems,
):
    me = lax.axis_index("seq")
    night = lax.axis_index("dp")
    core = me % 2
    chip = me // 2
    cx, cy = chip // 4, chip % 4
    ha = jnp.where(core == 0, cy, cx)
    qb = jnp.where(core == 0, cx, cy)
    half = cx // 2
    mate = me + 1 - 2 * core

    def place(a, b):
        return jnp.where(core == 0, (b * 4 + a) * 2, (a * 4 + b) * 2 + 1)

    def remote(src, dst, k, r, device):
        return pltpu.make_async_remote_copy(
            src_ref=src, dst_ref=dst, send_sem=send_sems.at[k], recv_sem=recv_sems.at[r],
            device_id=device, device_id_type=MESH,
        )

    barrier = pltpu.get_barrier_semaphore()

    def greet(device):
        pl.semaphore_signal(barrier, inc=1, device_id=device, device_id_type=MESH)

    def at(px, py, pc):
        return {"seq": (px * 4 + py) * 2 + pc}

    greet({"seq": mate})
    for d in range(1, 4):
        greet({"dp": (night + d) % 4})
        for pc in range(2):
            greet(at((cx + d) % 4, cy, pc))
            greet(at(cx, (cy + d) % 4, pc))
    own_copy = pltpu.make_async_copy(samples_hbm, own, sems.at[6])
    own_copy.start()
    shard_copy = pltpu.make_async_copy(shard, shard_buf, sems.at[7])
    shard_copy.start()
    copies = [
        pltpu.make_async_copy(middle_hbm.at[l], middle.at[l], sems.at[l]) for l in range(4)
    ]
    copies.append(pltpu.make_async_copy(last_hbm, last, sems.at[4]))
    copies.append(pltpu.make_async_copy(proj_hbm, proj, sems.at[5]))
    for copy in copies:
        copy.start()

    is_odd = core
    group_len = length[0, 0]
    even_len = jnp.where(is_odd == 1, 2 * FR - group_len, group_len)
    n1 = jnp.where(is_odd == 1, jnp.maximum(even_len - FR, 0), jnp.minimum(even_len, FR))
    own_rows = own.shape[0]

    def source(r):
        even = jnp.where(r < even_len, r, own_rows + r - even_len)
        odd = jnp.where(
            r + FR < even_len, own_rows + r + FR, r + FR - even_len
        )
        return jnp.where(is_odd == 1, odd, even)

    def picks(width, base, step):
        r = lax.broadcasted_iota(jnp.int32, (FR + TAIL, width), 0)
        col = lax.broadcasted_iota(jnp.int32, (FR + TAIL, width), 1) + base
        src = jnp.where(
            r < FR, source(r) + step, source(jnp.where(r == FR, n1 - 1, FR - 1)) + 1
        )
        return onehot(src == col)

    shard_copy.wait()
    gr = lax.broadcasted_iota(jnp.int32, (32, 20), 0)
    gc = lax.broadcasted_iota(jnp.int32, (32, 20), 1)
    zbuf[night] = dot(onehot(gr == gc), shard_buf[...]).astype(BF)
    own_copy.wait()
    pick_own = picks(own_rows, 0, 0)
    for c in range(0, 2560, 512):
        x[:, c : c + 512] = dot(pick_own, own[:, c : c + 512]).astype(BF)
    x[:, 2560:2688] = dot(picks(own_rows, 0, 1), own[:, :128]).astype(BF)
    for h in range(4):
        lanes_h = lax.broadcasted_iota(jnp.int32, (128, widen.shape[1]), 1)
        rows_h = lax.broadcasted_iota(jnp.int32, (128, widen.shape[1]), 0)
        widen[128 * h : 128 * h + 128, :] = onehot(
            (lanes_h == 320 * h + 80 * (rows_h // 20) + 60 + rows_h % 20) & (rows_h < 80)
        )
    mout[...] = jnp.zeros_like(mout)

    pl.semaphore_wait(barrier, 16)
    mine_z = zbuf.at[night]
    zcopies = [
        remote(mine_z, mine_z, 16 + d, 16 + (4 - d) % 4, {"dp": (night + d) % 4})
        for d in range(1, 4)
    ]
    for copy in zcopies:
        copy.start()
    swap = remote(samples_hbm, arr, 20, 20, {"seq": mate})
    swap.start()

    slot = me - 16 * half
    first_hops = []
    for d in range(4):
        ty, tx = (cy + d) % 4, (cx + d) % 4
        first_hops.append((
            at(cx, ty, half),
            remote(wblk.at[0], wbuf.at[0, slot], 48 + d, 48 + slot % 8, at(cx, ty, half)),
        ))
        first_hops.append((
            at(tx, cy, half),
            remote(
                wblk.at[1], wbuf.at[1, slot], 52 + d, 56 + (cx % 2) * 2 + core, at(tx, cy, half)
            ),
        ))
    def start_weights():
        for copy in zcopies:
            copy.wait_recv()
        cr = lax.broadcasted_iota(jnp.int32, (80, 128), 0)
        cc = lax.broadcasted_iota(jnp.int32, (80, 128), 1)
        packed = dot(
            onehot(cc == 32 * (cr // 20) + cr % 20), zbuf[...].reshape(128, zbuf.shape[2])
        ).astype(BF)
        wide = packed.shape[1] // 2
        wblk[0] = packed[:, :wide]
        wblk[1] = packed[:, wide:]
        for target, copy in first_hops:

            @pl.when(target["seq"] != me)
            def _():
                copy.start()

        @pl.when(half == core)
        def _():
            wbuf[0, slot] = wblk[0]
            wbuf[1, slot] = wblk[1]

    row_slots = pl.ds(8 * (cx % 2), 8)
    x_hops = [
        remote(
            wbuf.at[0, row_slots], wbuf.at[0, row_slots], 60 + d, 60 + cx % 2,
            at((cx + d) % 4, cy, core),
        )
        for d in range(1, 4)
    ]
    y_hops = [
        remote(
            wbuf.at[1, pl.ds(8 * p + 2 * cy, 2)], wbuf.at[1, pl.ds(8 * p + 2 * cy, 2)],
            64 + 2 * d + p, 64 + 2 * (4 - d) + p, at(cx, (cy + d) % 4, core),
        )
        for d in range(1, 4)
        for p in range(2)
    ]

    def second_hops():
        for k in range(8):

            @pl.when((half == core) & (k != slot % 8))
            def _():
                remote(
                    wblk.at[0], wbuf.at[0, 8 * (cx % 2) + k], 48, 48 + k, {"seq": mate}
                ).wait_recv()

        @pl.when(half == core)
        def _():
            for copy in x_hops:
                copy.start()

        for k in range(4):
            from_x, from_core = 2 * core + k // 2, k % 2

            @pl.when((from_x != cx) | (from_core != core))
            def _():
                remote(
                    wblk.at[1], wbuf.at[1, 8 * (k // 2) + 2 * cy + from_core], 52, 56 + k,
                    {"seq": mate},
                ).wait_recv()

        for copy in y_hops:
            copy.start()

    def weights_arrived():
        for p in range(2):

            @pl.when(2 * core + p != cx)
            def _():
                remote(
                    wbuf.at[0, pl.ds(8 * p, 8)], wbuf.at[0, pl.ds(8 * p, 8)], 60, 60 + p,
                    {"seq": mate},
                ).wait_recv()

        for d in range(1, 4):
            for p in range(2):
                block = wbuf.at[1, pl.ds(8 * p + 2 * ((cy + d) % 4), 2)]
                remote(block, block, 64, 64 + 2 * d + p, {"seq": mate}).wait_recv()

    def weights_sent():
        for target, copy in first_hops:

            @pl.when(target["seq"] != me)
            def _():
                copy.wait_send()

        @pl.when(half == core)
        def _():
            for copy in x_hops:
                copy.wait_send()

        for copy in y_hops:
            copy.wait_send()

    swap.wait_recv()
    pick_arr = picks(own_rows, own_rows, 0)
    for c in range(0, 2560, 512):
        x[:, c : c + 512] += dot(pick_arr, arr[:, c : c + 512]).astype(BF)
    x[:, 2560:2688] += dot(picks(own_rows, own_rows, 1), arr[:, :128]).astype(BF)

    nr = lax.broadcasted_iota(jnp.int32, (FR, FR + TAIL), 0)
    nc = lax.broadcasted_iota(jnp.int32, (FR, FR + TAIL), 1)
    following = jnp.where(nr == n1 - 1, FR, jnp.where(nr == FR - 1, FR + 1, nr + 1))
    pick_next = (following == nc).astype(F32).astype(BF)

    def close(a, t):
        body = jnp.concatenate([a[0, :, :CH], t[0, :, :CH]], axis=0)
        a[a.shape[0] - 1, :, :CH] = dot(pick_next, body).astype(BF)

    def layer_one(u, acc, parity, half):
        offset = lax.rem(40 * u, 128)
        base = pl.multiple_of(40 * u - offset, 128)
        er = lax.broadcasted_iota(jnp.int32, (256, 80), 0)
        ec = lax.broadcasted_iota(jnp.int32, (256, 80), 1)
        weight = dot((er == ec + offset).astype(F32).astype(BF), first[...]).astype(BF)
        parts = [x[:FR, pl.ds(pl.multiple_of(base + 640 * b, 128), 256)] for b in range(4)]
        parts.append(x[FR:, pl.ds(base, 256)])
        acc[...] = dot(jnp.concatenate(parts, axis=0), weight)

        def out(r, n, val):
            if r < 4 * FR:
                a1[8 * (r // FR) + half, r % FR : r % FR + n, parity * CH : parity * CH + CH] = val
            else:
                t1[half, :, parity * CH : parity * CH + CH] = val

        settle(acc, 4 * FR + TAIL, 1e-5, out)

    def one_step(i, carry):
        layer_one(2 * i, acc0, 0, i)
        layer_one(2 * i + 1, acc1, 1, i)
        return carry

    lax.fori_loop(0, 2, one_step, 0)
    start_weights()
    lax.fori_loop(2, 5, one_step, 0)
    second_hops()
    lax.fori_loop(5, 8, one_step, 0)
    close(a1, t1)

    def three_taps(ain, start, count, rows, layer, acc):
        pairs = ain[pl.ds(start, count)].reshape(count * rows, 2 * CH)
        ahead = ain[pl.ds(start + 1, count), :, :CH].reshape(count * rows, CH)
        acc[: count * rows, :] = dot(
            jnp.concatenate([pairs, ahead], axis=1), middle[layer]
        )

    def main_chunk(ain, aout, layer, i, acc):
        three_taps(ain, 4 * i, 4, FR, layer, acc)

        def out(r, n, val):
            s = r // FR
            aout[2 * i + s // 2, r % FR : r % FR + n, (s % 2) * CH : (s % 2) * CH + CH] = val

        settle(acc, 4 * FR, 2e-5, out)

    def tail_chunk(tin, tout, layer, count, acc):
        three_taps(tin, 0, count, TAIL, layer, acc)

        def out(r, n, val):
            for k in range(n // TAIL):
                s = (r + k * TAIL) // TAIL
                tout[s // 2, :, (s % 2) * CH : (s % 2) * CH + CH] = val[k * TAIL : (k + 1) * TAIL]

        settle(acc, count * TAIL, 2e-5, out)

    def layer(ain, aout, tin, tout, index, chunks, tail_count):
        copies[index].wait()

        def step(i, carry):
            main_chunk(ain, aout, index, 2 * i, acc0)
            main_chunk(ain, aout, index, 2 * i + 1, acc1)
            return carry

        if chunks > 1:
            lax.fori_loop(0, chunks // 2, step, 0)
        else:
            main_chunk(ain, aout, index, 0, acc0)
        if tail_count:
            tail_chunk(tin, tout, index, tail_count, acc1)
            close(aout, tout)

    layer(a1, a2, t1, t2, 0, 8, 7)
    layer(a2, a3, t2, t3, 1, 4, 3)
    layer(a3, a4, t3, t4, 2, 2, 1)
    layer(a4, a5, None, None, 3, 1, 0)

    copies[4].wait()
    acc0[: 2 * FR, :] = dot(a5[...].reshape(2 * FR, 2 * CH), last[0])

    def out6(r, n, val):
        a6[r % FR : r % FR + n, (r // FR) * CH : (r // FR) * CH + CH] = val

    settle(acc0, 2 * FR, 2e-5, out6)
    acc1[:FR, :] = dot(a6[...], last[1])
    feats = []
    settle(acc1, FR, 2e-5, lambda r, n, val: feats.append(val))
    frame_feat = jnp.concatenate(feats, axis=0).astype(F32)
    normed_feat = (row_norm(frame_feat, 2e-5) * gain[...]).astype(BF)
    copies[5].wait()
    hidden = (dot(normed_feat, proj[...]) + bias[...]).astype(BF)
    hidden_buf[...] = hidden
    normed2[pl.ds(pl.multiple_of(core * FR, FR), FR), :] = (
        row_norm(hidden.astype(F32), 1e-5) * attn_gain[...]
    ).astype(BF)
    mine = normed2.at[pl.ds(pl.multiple_of(core * FR, FR), FR)]
    exchange = remote(mine, mine, 21, 21, {"seq": mate})
    exchange.start()
    weights_arrived()
    exchange.wait_recv()

    def head_weights(h):
        return jnp.concatenate(
            [wbuf[p, pl.ds(4 * h, 4)].reshape(320, wbuf.shape[3]) for p in range(2)], axis=1
        )

    yr = lax.broadcasted_iota(jnp.int32, (320, 1), 0)
    row_scale = jnp.where(yr % 80 < 20, SCALE, 1.0).astype(F32)
    pr = lax.broadcasted_iota(jnp.int32, (240, 320), 0)
    pc = lax.broadcasted_iota(jnp.int32, (240, 320), 1)
    regroup = onehot(pc == 80 * ((pr % 80) // 20) + 20 * (pr // 80) + pr % 20)

    def project(h, carry):
        y = lax.dot_general(head_weights(h), normed2[...], NT, preferred_element_type=F32)
        ysend[h] = dot(regroup, (y * row_scale).astype(BF)).astype(BF)
        return carry

    forwards = []

    def forward(d, block):
        for e in range(1, 4):
            copy = remote(
                block.at[pl.ds(80, 160)], kvbuf.at[qb, (ha + d) % 4],
                28 + 4 * d + e, 28 + 4 * d + (4 - e) % 4, {"seq": place(ha, (qb + e) % 4)},
            )
            copy.start()
            forwards.append(copy)

    heads = []
    for d in (0, 1, 3, 2):
        to = (ha + d) % 4
        project(to, 0)
        if d == 0:
            forward(0, ysend.at[ha])
            continue
        heads.append(
            remote(ysend.at[to], qkv.at[ha], 24 + d, 24 + (4 - d) % 4, {"seq": place(to, qb)})
        )
        heads[-1].start()
    qkv[ha] = ysend[ha]
    for d in (3, 1, 2):
        remote(ysend.at[0], qkv.at[(ha + d) % 4], 24, 24 + d, {"seq": mate}).wait_recv()
        forward(d, qkv.at[(ha + d) % 4])

    for i in range(4):
        qs[i] = jnp.transpose(qkv[i, :80, :].astype(F32)).astype(BF)

    def masses(values):
        ones = jnp.ones((16, values.shape[1]), BF)
        return jnp.concatenate([values, ones], axis=0)

    def attend(keys, values, is_first, finish=None):
        def step(i, carry):
            s = dot(qs[i], keys)
            top = jnp.max(s, axis=-1, keepdims=True)
            if not is_first:
                top = jnp.maximum(top, peak[i])
            p = jnp.exp2(s - top)
            o = lax.dot_general(p.astype(BF), masses(values), NT, preferred_element_type=F32)
            if not is_first:
                fade = jnp.exp2(peak[i] - top)
                o = o + accum[i] * fade
            peak[i] = top
            accum[i] = o
            return carry

        if finish is None:
            lax.fori_loop(0, 2, lambda i, c: step(2 * i + 1, step(2 * i, c)), 0)
        else:
            for d in (1, 2, 3, 0):
                step((ha + d) % 4, 0)
                finish(d)

    returns = []
    keep2 = pltpu.make_async_copy(mout.at[ha], mbuf.at[ha], sems.at[9])

    def give_back(d):
        to = (ha + d) % 4
        mout[to, :, :80] = (accum[to, :, :80] / accum[to, :, 80:81]).astype(BF)
        if d == 0:
            keep2.start()
        else:
            returns.append(
                remote(mout.at[to], mbuf.at[ha], 44 + d, 44 + (4 - d) % 4, {"seq": place(to, qb)})
            )
            returns[-1].start()

    for d in (0, 3, 1, 2):
        a = (ha + d) % 4
        for e in range(1, 4):
            remote(
                qkv.at[0, pl.ds(80, 160)], kvbuf.at[(qb + e) % 4, a], 28, 28 + 4 * d + e,
                {"seq": mate},
            ).wait_recv()
        blocks = [qkv[a, 80:, :]] + [kvbuf[(qb + e) % 4, a] for e in range(1, 4)]
        attend(
            jnp.concatenate([block[:80] for block in blocks], axis=1),
            jnp.concatenate([block[80:] for block in blocks], axis=1),
            d == 0,
            give_back if d == 2 else None,
        )
    keep2.wait()
    for d in range(1, 4):
        remote(mout.at[0], mbuf.at[(ha + d) % 4], 44, 44 + d, {"seq": mate}).wait_recv()

    def output(rows_of):
        rows = pl.ds(pl.multiple_of(rows_of * FR, FR), FR)
        mixed = jnp.concatenate([mbuf[h, rows, :] for h in range(4)], axis=1)
        wide = dot(mixed, widen[...]).astype(BF)
        return jnp.concatenate(
            [dot(wide, wbuf[p].reshape(1280, wbuf.shape[3])) for p in range(2)], axis=1
        )

    psend[...] = output(1 - core).astype(BF)
    last_swap = remote(psend, precv, 22, 22, {"seq": mate})
    last_swap.start()
    base = hidden_buf[...].astype(F32) + output(core)
    last_swap.wait_recv()
    out_ref[...] = (base + precv[...].astype(F32)).astype(BF)

    for copy in [swap, exchange, last_swap] + zcopies + heads + forwards + returns:
        copy.wait_send()
    weights_sent()


def call(length, samples, shard, first, middle, last, gain, proj, bias, attn_gain):
    vmem = pl.BlockSpec(memory_space=pltpu.VMEM)
    hbm = pl.BlockSpec(memory_space=pl.ANY)
    rows, block = samples.shape
    width = proj.shape[1]
    return pl.pallas_call(
        kernel,
        out_shape=jax.ShapeDtypeStruct((FR, width), BF),
        in_specs=[
            pl.BlockSpec(memory_space=pltpu.SMEM), hbm, hbm, vmem, hbm, hbm, vmem, hbm, vmem, vmem,
        ],
        out_specs=vmem,
        scratch_shapes=[
            pltpu.VMEM((rows, block), BF),
            pltpu.VMEM((rows, block), BF),
            pltpu.VMEM((FR + TAIL, block + 128), BF),
            pltpu.VMEM((33, FR, 2 * CH), BF),
            pltpu.VMEM((17, FR, 2 * CH), BF),
            pltpu.VMEM((9, FR, 2 * CH), BF),
            pltpu.VMEM((5, FR, 2 * CH), BF),
            pltpu.VMEM((2, FR, 2 * CH), BF),
            pltpu.VMEM((FR, 2 * CH), BF),
            pltpu.VMEM((8, TAIL, 2 * CH), BF),
            pltpu.VMEM((4, TAIL, 2 * CH), BF),
            pltpu.VMEM((2, TAIL, 2 * CH), BF),
            pltpu.VMEM((1, TAIL, 2 * CH), BF),
            pltpu.VMEM((4 * FR + TAIL, CH), F32),
            pltpu.VMEM((4 * FR + TAIL, CH), F32),
            pltpu.VMEM(middle.shape, BF),
            pltpu.VMEM(last.shape, BF),
            pltpu.VMEM(proj.shape, BF),
            pltpu.VMEM((20, width), BF),
            pltpu.VMEM((4, 32, width), BF),
            pltpu.VMEM((2, 80, width // 2), BF),
            pltpu.VMEM((2, 16, 80, width // 2), BF),
            pltpu.VMEM((2 * FR, width), BF),
            pltpu.VMEM((FR, width), BF),
            pltpu.VMEM((4, 240, 256), BF),
            pltpu.VMEM((4, 240, 256), BF),
            pltpu.VMEM((4, 4, 160, 256), BF),
            pltpu.VMEM((4, 256, 80), BF),
            pltpu.VMEM((4, 256, 1), F32),
            pltpu.VMEM((4, 256, 96), F32),
            pltpu.VMEM((4, 256, 128), BF),
            pltpu.VMEM((4, 256, 128), BF),
            pltpu.VMEM((512, width), BF),
            pltpu.VMEM((FR, width), BF),
            pltpu.VMEM((FR, width), BF),
            pltpu.SemaphoreType.DMA((10,)),
            pltpu.SemaphoreType.DMA((72,)),
            pltpu.SemaphoreType.DMA((72,)),
        ],
        compiler_params=pltpu.CompilerParams(
            vmem_limit_bytes=60 << 20, collective_id=0, has_side_effects=True
        ),
        cost_estimate=pl.CostEstimate(
            flops=20 * 10**9, bytes_accessed=20 * 10**6, transcendentals=13 * 10**6
        ),
        name="encoder",
    )(
        length, samples, shard, first, middle, last, gain, proj, bias,
        attn_gain,
    )


def body(
    group_samples, group_lengths, group_offsets, conv_first, conv_middle, conv_last,
    feat_gain, proj_weight, proj_bias, attn_gain, attn_weight,
):
    encoded = call(
        group_lengths, group_samples[0, 0], attn_weight.T, conv_first, conv_middle, conv_last,
        feat_gain, proj_weight, proj_bias, attn_gain,
    )
    return encoded.reshape(1, FR, -1)


def solution(mesh):
    in_specs = (
        P("dp", "seq", None, None), P("dp", "seq"), P("dp", "seq"),
        P(), P(), P(), P(), P(), P(), P(), P(None, ("dp", "seq")),
    )
    out_specs = P("dp", "seq", None)
    return jax.shard_map(body, mesh=mesh, in_specs=in_specs, out_specs=out_specs, check_vma=False)
```

```python
import math

import jax
import jax.numpy as jnp
from jax import lax
from jax.experimental import pallas as pl
from jax.experimental.pallas import tpu as pltpu
from jax.sharding import PartitionSpec as P

FR = 128
CH = 512
TAIL = 16
SWAP = 80
BF = jnp.bfloat16
F32 = jnp.float32
SCALE = math.log2(math.e) / math.sqrt(80)


def dot(a, b):
    return jnp.dot(a, b, preferred_element_type=F32)


def row_norm(v, eps):
    center = jnp.mean(v, axis=-1, keepdims=True)
    d = v - center
    spread = jnp.mean(d * d, axis=-1, keepdims=True)
    return d * lax.rsqrt(spread + eps)


def settle(acc, rows, eps, out):
    for r in range(0, rows, 64):
        n = min(64, rows - r)
        v = acc[r : r + n, :]
        center = jnp.mean(v, axis=-1, keepdims=True)
        d = v - center
        spread = jnp.mean(d * d, axis=-1, keepdims=True)
        u = d * lax.rsqrt(2.0 * spread + 2.0 * eps)
        out(r, n, (u + u * lax.erf(u)).astype(BF))


MESH = pl.DeviceIdType.MESH
NT = (((1,), (1,)), ((), ()))


def onehot(mask):
    return mask.astype(F32).astype(BF)


def kernel(
    length, samples_hbm, shard, first, middle_hbm, last_hbm, gain, proj_hbm, bias, attn_gain,
    out_ref,
    own, outgoing, arr, x, a1, a2, a3, a4, a5, a6, t1, t2, t3, t4, acc0, acc1, middle, last, proj,
    shifted, acc2, acc3, shard_buf, zbuf, wblk, wbuf, normed2, hidden_buf, ysend, qkv, kvbuf, qs, peak, accum,
    mout, mbuf, out_weight, psend, precv, sems, send_sems, recv_sems,
):
    me = lax.axis_index("seq")
    night = lax.axis_index("dp")
    core = me % 2
    chip = me // 2
    cx, cy = chip // 4, chip % 4
    ha = jnp.where(core == 0, cy, cx)
    qb = jnp.where(core == 0, cx, cy)
    half = cx // 2
    mate = me + 1 - 2 * core

    def place(a, b):
        return jnp.where(core == 0, (b * 4 + a) * 2, (a * 4 + b) * 2 + 1)

    def remote(src, dst, k, r, device):
        return pltpu.make_async_remote_copy(
            src_ref=src, dst_ref=dst, send_sem=send_sems.at[k], recv_sem=recv_sems.at[r],
            device_id=device, device_id_type=MESH,
        )

    barrier = pltpu.get_barrier_semaphore()

    def greet(device):
        pl.semaphore_signal(barrier, inc=1, device_id=device, device_id_type=MESH)

    def at(px, py, pc):
        return {"seq": (px * 4 + py) * 2 + pc}

    greet({"seq": mate})
    for d in range(1, 4):
        greet({"dp": (night + d) % 4})
        for pc in range(2):
            greet(at((cx + d) % 4, cy, pc))
            greet(at(cx, (cy + d) % 4, pc))
    own_copy = pltpu.make_async_copy(samples_hbm, own, sems.at[6])
    own_copy.start()
    shard_copy = pltpu.make_async_copy(shard, shard_buf, sems.at[7])
    shard_copy.start()
    copies = [
        pltpu.make_async_copy(middle_hbm.at[l], middle.at[l], sems.at[l]) for l in range(4)
    ]
    copies.append(pltpu.make_async_copy(last_hbm, last, sems.at[4]))
    copies.append(pltpu.make_async_copy(proj_hbm, proj, sems.at[5]))
    for copy in copies:
        copy.start()

    is_odd = core
    group_len = length[0, 0]
    even_len = jnp.where(is_odd == 1, 2 * FR - group_len, group_len)
    n1 = jnp.where(is_odd == 1, jnp.maximum(even_len - FR, 0), jnp.minimum(even_len, FR))
    own_rows = own.shape[0]

    def source(r):
        even = jnp.where(r < even_len, r, own_rows + r - even_len)
        odd = jnp.where(
            r + FR < even_len, own_rows + r + FR - (own_rows - SWAP), r + FR - even_len
        )
        return jnp.where(is_odd == 1, odd, even)

    def picks(width, base, step):
        r = lax.broadcasted_iota(jnp.int32, (FR + TAIL, width), 0)
        col = lax.broadcasted_iota(jnp.int32, (FR + TAIL, width), 1) + base
        src = jnp.where(
            r < FR, source(r) + step, source(jnp.where(r == FR, n1 - 1, FR - 1)) + 1
        )
        return onehot(src == col)

    shard_copy.wait()
    gr = lax.broadcasted_iota(jnp.int32, (32, 20), 0)
    gc = lax.broadcasted_iota(jnp.int32, (32, 20), 1)
    zbuf[night] = dot(onehot(gr == gc), shard_buf[...]).astype(BF)
    own_copy.wait()
    sr = lax.broadcasted_iota(jnp.int32, (SWAP, own_rows), 0)
    sc = lax.broadcasted_iota(jnp.int32, (SWAP, own_rows), 1)
    pick_swap = onehot(sc == sr + jnp.where(core == 0, own_rows - SWAP, 0))
    for c in range(0, 2560, 512):
        outgoing[:, c : c + 512] = dot(pick_swap, own[:, c : c + 512]).astype(BF)
    pl.semaphore_wait(barrier, 16)
    swap = remote(outgoing, arr, 20, 20, {"seq": mate})
    swap.start()
    mine_z = zbuf.at[night]
    zcopies = [
        remote(mine_z, mine_z, 16 + d, 16 + (4 - d) % 4, {"dp": (night + d) % 4})
        for d in range(1, 4)
    ]
    for copy in zcopies:
        copy.start()
    pick_own = picks(own_rows, 0, 0)
    for c in range(0, 2560, 512):
        x[:, c : c + 512] = dot(pick_own, own[:, c : c + 512]).astype(BF)
    x[:, 2560:2688] = dot(picks(own_rows, 0, 1), own[:, :128]).astype(BF)
    mout[...] = jnp.zeros_like(mout)
    er = lax.broadcasted_iota(jnp.int32, (256, 80), 0)
    ec = lax.broadcasted_iota(jnp.int32, (256, 80), 1)

    def shift(u, carry):
        shifted[u] = dot(onehot(er == ec + lax.rem(40 * u, 128)), first[...]).astype(BF)
        return carry

    lax.fori_loop(0, 16, shift, 0)

    slot = me - 16 * half
    first_hops = []
    for d in range(4):
        ty, tx = (cy + d) % 4, (cx + d) % 4
        first_hops.append((
            at(cx, ty, half),
            remote(wblk.at[0], wbuf.at[0, slot], 48 + d, 48 + slot % 8, at(cx, ty, half)),
        ))
        first_hops.append((
            at(tx, cy, half),
            remote(
                wblk.at[1], wbuf.at[1, slot], 52 + d, 56 + (cx % 2) * 2 + core, at(tx, cy, half)
            ),
        ))
    def start_weights():
        for copy in zcopies:
            copy.wait_recv()
        cr = lax.broadcasted_iota(jnp.int32, (80, 128), 0)
        cc = lax.broadcasted_iota(jnp.int32, (80, 128), 1)
        packed = dot(
            onehot(cc == 32 * (cr // 20) + cr % 20), zbuf[...].reshape(128, zbuf.shape[2])
        ).astype(BF)
        wide = packed.shape[1] // 2
        wblk[0] = packed[:, :wide]
        wblk[1] = packed[:, wide:]
        for target, copy in first_hops:

            @pl.when(target["seq"] != me)
            def _():
                copy.start()

        @pl.when(half == core)
        def _():
            wbuf[0, slot] = wblk[0]
            wbuf[1, slot] = wblk[1]

    row_slots = pl.ds(8 * (cx % 2), 8)
    x_hops = [
        remote(
            wbuf.at[0, row_slots], wbuf.at[0, row_slots], 60 + d, 60 + cx % 2,
            at((cx + d) % 4, cy, core),
        )
        for d in (2, 1, 3)
    ]
    y_hops = [
        remote(
            wbuf.at[1, pl.ds(8 * p + 2 * cy, 2)], wbuf.at[1, pl.ds(8 * p + 2 * cy, 2)],
            64 + 2 * d + p, 64 + 2 * (4 - d) + p, at(cx, (cy + d) % 4, core),
        )
        for d in (2, 1, 3)
        for p in range(2)
    ]

    def second_hops():
        for k in range(8):

            @pl.when((half == core) & (k != slot % 8))
            def _():
                remote(
                    wblk.at[0], wbuf.at[0, 8 * (cx % 2) + k], 48, 48 + k, {"seq": mate}
                ).wait_recv()

        @pl.when(half == core)
        def _():
            for copy in x_hops:
                copy.start()

        for k in range(4):
            from_x, from_core = 2 * core + k // 2, k % 2

            @pl.when((from_x != cx) | (from_core != core))
            def _():
                remote(
                    wblk.at[1], wbuf.at[1, 8 * (k // 2) + 2 * cy + from_core], 52, 56 + k,
                    {"seq": mate},
                ).wait_recv()

        for copy in y_hops:
            copy.start()

    def weights_arrived():
        for p in range(2):

            @pl.when(2 * core + p != cx)
            def _():
                remote(
                    wbuf.at[0, pl.ds(8 * p, 8)], wbuf.at[0, pl.ds(8 * p, 8)], 60, 60 + p,
                    {"seq": mate},
                ).wait_recv()

        for d in range(1, 4):
            for p in range(2):
                block = wbuf.at[1, pl.ds(8 * p + 2 * ((cy + d) % 4), 2)]
                remote(block, block, 64, 64 + 2 * d + p, {"seq": mate}).wait_recv()

    def weights_sent():
        for target, copy in first_hops:

            @pl.when(target["seq"] != me)
            def _():
                copy.wait_send()

        @pl.when(half == core)
        def _():
            for copy in x_hops:
                copy.wait_send()

        for copy in y_hops:
            copy.wait_send()

    swap.wait_recv()
    pick_arr = picks(SWAP, own_rows, 0)
    for c in range(0, 2560, 512):
        x[:, c : c + 512] += dot(pick_arr, arr[:, c : c + 512]).astype(BF)
    x[:, 2560:2688] += dot(picks(SWAP, own_rows, 1), arr[:, :128]).astype(BF)

    nr = lax.broadcasted_iota(jnp.int32, (FR, FR + TAIL), 0)
    nc = lax.broadcasted_iota(jnp.int32, (FR, FR + TAIL), 1)
    following = jnp.where(nr == n1 - 1, FR, jnp.where(nr == FR - 1, FR + 1, nr + 1))
    pick_next = (following == nc).astype(F32).astype(BF)

    def close(a, t):
        body = jnp.concatenate([a[0, :, :CH], t[0, :, :CH]], axis=0)
        a[a.shape[0] - 1, :, :CH] = dot(pick_next, body).astype(BF)

    def layer_one(u, acc, parity, half):
        offset = lax.rem(40 * u, 128)
        base = pl.multiple_of(40 * u - offset, 128)
        parts = [x[:FR, pl.ds(pl.multiple_of(base + 640 * b, 128), 256)] for b in range(4)]
        parts.append(x[FR:, pl.ds(base, 256)])
        acc[...] = dot(jnp.concatenate(parts, axis=0), shifted[u])

        def out(r, n, val):
            if r < 4 * FR:
                a1[8 * (r // FR) + half, r % FR : r % FR + n, parity * CH : parity * CH + CH] = val
            else:
                t1[half, :, parity * CH : parity * CH + CH] = val

        settle(acc, 4 * FR + TAIL, 1e-5, out)

    def one_step(i, carry):
        for k, acc in enumerate((acc0, acc1, acc2, acc3)):
            layer_one(4 * i + k, acc, k % 2, 2 * i + k // 2)
        return carry

    lax.fori_loop(0, 1, one_step, 0)
    start_weights()
    lax.fori_loop(1, 4, one_step, 0)
    second_hops()
    close(a1, t1)

    def three_taps(ain, start, count, rows, layer, acc):
        pairs = ain[pl.ds(start, count)].reshape(count * rows, 2 * CH)
        ahead = ain[pl.ds(start + 1, count), :, :CH].reshape(count * rows, CH)
        acc[: count * rows, :] = dot(
            jnp.concatenate([pairs, ahead], axis=1), middle[layer]
        )

    def main_chunk(ain, aout, layer, i, acc):
        three_taps(ain, 4 * i, 4, FR, layer, acc)

        def out(r, n, val):
            s = r // FR
            aout[2 * i + s // 2, r % FR : r % FR + n, (s % 2) * CH : (s % 2) * CH + CH] = val

        settle(acc, 4 * FR, 2e-5, out)

    def tail_chunk(tin, tout, layer, count, acc):
        three_taps(tin, 0, count, TAIL, layer, acc)

        def out(r, n, val):
            for k in range(n // TAIL):
                s = (r + k * TAIL) // TAIL
                tout[s // 2, :, (s % 2) * CH : (s % 2) * CH + CH] = val[k * TAIL : (k + 1) * TAIL]

        settle(acc, count * TAIL, 2e-5, out)

    def layer(ain, aout, tin, tout, index, chunks, tail_count):
        copies[index].wait()

        def step(i, carry):
            for k, acc in enumerate((acc0, acc1, acc2, acc3)):
                main_chunk(ain, aout, index, 4 * i + k, acc)
            return carry

        if chunks >= 4:
            lax.fori_loop(0, chunks // 4, step, 0)
        else:
            for k in range(chunks):
                main_chunk(ain, aout, index, k, (acc0, acc1)[k])
        if tail_count:
            tail_chunk(tin, tout, index, tail_count, acc2)
            close(aout, tout)

    layer(a1, a2, t1, t2, 0, 8, 7)
    layer(a2, a3, t2, t3, 1, 4, 3)
    layer(a3, a4, t3, t4, 2, 2, 1)
    layer(a4, a5, None, None, 3, 1, 0)

    copies[4].wait()
    acc0[: 2 * FR, :] = dot(a5[...].reshape(2 * FR, 2 * CH), last[0])

    def out6(r, n, val):
        a6[r % FR : r % FR + n, (r // FR) * CH : (r // FR) * CH + CH] = val

    settle(acc0, 2 * FR, 2e-5, out6)
    acc1[:FR, :] = dot(a6[...], last[1])
    feats = []
    settle(acc1, FR, 2e-5, lambda r, n, val: feats.append(val))
    frame_feat = jnp.concatenate(feats, axis=0).astype(F32)
    normed_feat = (row_norm(frame_feat, 2e-5) * gain[...]).astype(BF)
    copies[5].wait()
    hidden = (dot(normed_feat, proj[...]) + bias[...]).astype(BF)
    hidden_buf[...] = hidden
    normed2[pl.ds(pl.multiple_of(core * FR, FR), FR), :] = (
        row_norm(hidden.astype(F32), 1e-5) * attn_gain[...]
    ).astype(BF)
    mine = normed2.at[pl.ds(pl.multiple_of(core * FR, FR), FR)]
    exchange = remote(mine, mine, 21, 21, {"seq": mate})
    exchange.start()
    weights_arrived()
    exchange.wait_recv()

    def head_weights(h):
        return jnp.concatenate(
            [wbuf[p, pl.ds(4 * h, 4)].reshape(320, wbuf.shape[3]) for p in range(2)], axis=1
        )

    yr = lax.broadcasted_iota(jnp.int32, (320, 1), 0)
    row_scale = jnp.where(yr % 80 < 20, SCALE, 1.0).astype(F32)
    pr = lax.broadcasted_iota(jnp.int32, (240, 320), 0)
    pc = lax.broadcasted_iota(jnp.int32, (240, 320), 1)
    regroup = onehot(pc == 80 * ((pr % 80) // 20) + 20 * (pr // 80) + pr % 20)

    def project(h, carry):
        y = lax.dot_general(head_weights(h), normed2[...], NT, preferred_element_type=F32)
        ysend[h] = dot(regroup, (y * row_scale).astype(BF)).astype(BF)
        return carry

    forwards = []

    def forward(d, block):
        for e in range(1, 4):
            copy = remote(
                block.at[pl.ds(80, 160)], kvbuf.at[qb, (ha + d) % 4],
                28 + 4 * d + e, 28 + 4 * d + (4 - e) % 4, {"seq": place(ha, (qb + e) % 4)},
            )
            copy.start()
            forwards.append(copy)

    heads = []
    for d in (0, 1, 3, 2):
        to = (ha + d) % 4
        project(to, 0)
        if d == 0:
            forward(0, ysend.at[ha])
            continue
        heads.append(
            remote(ysend.at[to], qkv.at[ha], 24 + d, 24 + (4 - d) % 4, {"seq": place(to, qb)})
        )
        heads[-1].start()
    qkv[ha] = ysend[ha]
    wr = lax.broadcasted_iota(jnp.int32, (128, 320), 0)
    wc = lax.broadcasted_iota(jnp.int32, (128, 320), 1)
    pick_out = onehot((wc == 80 * (wr // 20) + 60 + wr % 20) & (wr < 80))
    for h in range(4):
        out_weight[128 * h : 128 * h + 128, :] = dot(pick_out, head_weights(h)).astype(BF)
    for d in (3, 1, 2):
        remote(ysend.at[0], qkv.at[(ha + d) % 4], 24, 24 + d, {"seq": mate}).wait_recv()
        forward(d, qkv.at[(ha + d) % 4])

    for i in range(4):
        qs[i] = jnp.transpose(qkv[i, :80, :].astype(F32)).astype(BF)

    def masses(values):
        ones = jnp.ones((16, values.shape[1]), BF)
        return jnp.concatenate([values, ones], axis=0)

    def attend(keys, values, is_first, finish=None):
        def step(i, carry):
            s = dot(qs[i], keys)
            top = jnp.max(s, axis=-1, keepdims=True)
            if not is_first:
                top = jnp.maximum(top, peak[i])
            p = jnp.exp2(s - top)
            o = lax.dot_general(p.astype(BF), masses(values), NT, preferred_element_type=F32)
            if not is_first:
                fade = jnp.exp2(peak[i] - top)
                o = o + accum[i] * fade
            peak[i] = top
            accum[i] = o
            return carry

        if finish is None:
            for i in range(4):
                step(i, 0)
        else:
            for d in (1, 2, 3, 0):
                step((ha + d) % 4, 0)
                finish(d)

    returns = []
    keep2 = pltpu.make_async_copy(mout.at[ha], mbuf.at[ha], sems.at[9])

    def give_back(d):
        to = (ha + d) % 4
        mout[to, :, :80] = (accum[to, :, :80] / accum[to, :, 80:81]).astype(BF)
        if d == 0:
            keep2.start()
        else:
            returns.append(
                remote(mout.at[to], mbuf.at[ha], 44 + d, 44 + (4 - d) % 4, {"seq": place(to, qb)})
            )
            returns[-1].start()

    for d in (0, 3, 1, 2):
        a = (ha + d) % 4
        for e in range(1, 4):
            remote(
                qkv.at[0, pl.ds(80, 160)], kvbuf.at[(qb + e) % 4, a], 28, 28 + 4 * d + e,
                {"seq": mate},
            ).wait_recv()
        blocks = [qkv[a, 80:, :]] + [kvbuf[(qb + e) % 4, a] for e in range(1, 4)]
        attend(
            jnp.concatenate([block[:80] for block in blocks], axis=1),
            jnp.concatenate([block[80:] for block in blocks], axis=1),
            d == 0,
            give_back if d == 2 else None,
        )
    keep2.wait()
    for d in range(1, 4):
        remote(mout.at[0], mbuf.at[(ha + d) % 4], 44, 44 + d, {"seq": mate}).wait_recv()

    def output(rows_of):
        rows = pl.ds(pl.multiple_of(rows_of * FR, FR), FR)
        mixed = jnp.concatenate([mbuf[h, rows, :] for h in range(4)], axis=1)
        return dot(mixed, out_weight[...])

    psend[...] = output(1 - core).astype(BF)
    last_swap = remote(psend, precv, 22, 22, {"seq": mate})
    last_swap.start()
    base = hidden_buf[...].astype(F32) + output(core)
    last_swap.wait_recv()
    out_ref[...] = (base + precv[...].astype(F32)).astype(BF)

    for copy in [swap, exchange, last_swap] + zcopies + heads + forwards + returns:
        copy.wait_send()
    weights_sent()


def call(length, samples, shard, first, middle, last, gain, proj, bias, attn_gain):
    vmem = pl.BlockSpec(memory_space=pltpu.VMEM)
    hbm = pl.BlockSpec(memory_space=pl.ANY)
    rows, block = samples.shape
    width = proj.shape[1]
    return pl.pallas_call(
        kernel,
        out_shape=jax.ShapeDtypeStruct((FR, width), BF),
        in_specs=[
            pl.BlockSpec(memory_space=pltpu.SMEM), hbm, hbm, vmem, hbm, hbm, vmem, hbm, vmem, vmem,
        ],
        out_specs=vmem,
        scratch_shapes=[
            pltpu.VMEM((rows, block), BF),
            pltpu.VMEM((SWAP, block), BF),
            pltpu.VMEM((SWAP, block), BF),
            pltpu.VMEM((FR + TAIL, block + 128), BF),
            pltpu.VMEM((33, FR, 2 * CH), BF),
            pltpu.VMEM((17, FR, 2 * CH), BF),
            pltpu.VMEM((9, FR, 2 * CH), BF),
            pltpu.VMEM((5, FR, 2 * CH), BF),
            pltpu.VMEM((2, FR, 2 * CH), BF),
            pltpu.VMEM((FR, 2 * CH), BF),
            pltpu.VMEM((8, TAIL, 2 * CH), BF),
            pltpu.VMEM((4, TAIL, 2 * CH), BF),
            pltpu.VMEM((2, TAIL, 2 * CH), BF),
            pltpu.VMEM((1, TAIL, 2 * CH), BF),
            pltpu.VMEM((4 * FR + TAIL, CH), F32),
            pltpu.VMEM((4 * FR + TAIL, CH), F32),
            pltpu.VMEM(middle.shape, BF),
            pltpu.VMEM(last.shape, BF),
            pltpu.VMEM(proj.shape, BF),
            pltpu.VMEM((16, 256, CH), BF),
            pltpu.VMEM((4 * FR + TAIL, CH), F32),
            pltpu.VMEM((4 * FR + TAIL, CH), F32),
            pltpu.VMEM((20, width), BF),
            pltpu.VMEM((4, 32, width), BF),
            pltpu.VMEM((2, 80, width // 2), BF),
            pltpu.VMEM((2, 16, 80, width // 2), BF),
            pltpu.VMEM((2 * FR, width), BF),
            pltpu.VMEM((FR, width), BF),
            pltpu.VMEM((4, 240, 256), BF),
            pltpu.VMEM((4, 240, 256), BF),
            pltpu.VMEM((4, 4, 160, 256), BF),
            pltpu.VMEM((4, 256, 80), BF),
            pltpu.VMEM((4, 256, 1), F32),
            pltpu.VMEM((4, 256, 96), F32),
            pltpu.VMEM((4, 256, 128), BF),
            pltpu.VMEM((4, 256, 128), BF),
            pltpu.VMEM((512, width), BF),
            pltpu.VMEM((FR, width), BF),
            pltpu.VMEM((FR, width), BF),
            pltpu.SemaphoreType.DMA((10,)),
            pltpu.SemaphoreType.DMA((72,)),
            pltpu.SemaphoreType.DMA((72,)),
        ],
        compiler_params=pltpu.CompilerParams(
            vmem_limit_bytes=60 << 20, collective_id=0, has_side_effects=True
        ),
        cost_estimate=pl.CostEstimate(
            flops=20 * 10**9, bytes_accessed=20 * 10**6, transcendentals=13 * 10**6
        ),
        name="encoder",
    )(
        length, samples, shard, first, middle, last, gain, proj, bias,
        attn_gain,
    )


def body(
    group_samples, group_lengths, group_offsets, conv_first, conv_middle, conv_last,
    feat_gain, proj_weight, proj_bias, attn_gain, attn_weight,
):
    encoded = call(
        group_lengths, group_samples[0, 0], attn_weight.T, conv_first, conv_middle, conv_last,
        feat_gain, proj_weight, proj_bias, attn_gain,
    )
    return encoded.reshape(1, FR, -1)


def solution(mesh):
    in_specs = (
        P("dp", "seq", None, None), P("dp", "seq"), P("dp", "seq"),
        P(), P(), P(), P(), P(), P(), P(), P(None, ("dp", "seq")),
    )
    out_specs = P("dp", "seq", None)
    return jax.shard_map(body, mesh=mesh, in_specs=in_specs, out_specs=out_specs, check_vma=False)
```

```python
import math

import jax
import jax.numpy as jnp
from jax import lax
from jax.experimental import pallas as pl
from jax.experimental.pallas import tpu as pltpu
from jax.sharding import PartitionSpec as P

FR = 128
CH = 512
TAIL = 16
SWAP = 80
BF = jnp.bfloat16
F32 = jnp.float32
SCALE = math.log2(math.e) / math.sqrt(80)


def dot(a, b):
    return jnp.dot(a, b, preferred_element_type=F32)


def row_norm(v, eps):
    center = jnp.mean(v, axis=-1, keepdims=True)
    d = v - center
    spread = jnp.mean(d * d, axis=-1, keepdims=True)
    return d * lax.rsqrt(spread + eps)


def settle(acc, rows, eps, out):
    for r in range(0, rows, 64):
        n = min(64, rows - r)
        v = acc[r : r + n, :]
        center = jnp.mean(v, axis=-1, keepdims=True)
        d = v - center
        spread = jnp.mean(d * d, axis=-1, keepdims=True)
        u = d * lax.rsqrt(2.0 * spread + 2.0 * eps)
        out(r, n, (u + u * lax.erf(u)).astype(BF))


MESH = pl.DeviceIdType.MESH
NT = (((1,), (1,)), ((), ()))


def onehot(mask):
    return mask.astype(F32).astype(BF)


def kernel(
    length, samples_hbm, shard, first, middle_hbm, last_hbm, gain, proj_hbm, bias, attn_gain,
    out_ref,
    own, outgoing, arr, x, a1, a2, a3, a4, a5, a6, t1, t2, t3, t4, acc0, acc1, middle, last, proj,
    shifted, acc2, acc3, shard_buf, zbuf, wblk, wbuf, normed2, hidden_buf, ysend, qkv, kvbuf, qs, peak, accum,
    mout, mbuf, out_weight, psend, precv, sems, send_sems, recv_sems,
):
    me = lax.axis_index("seq")
    night = lax.axis_index("dp")
    core = me % 2
    chip = me // 2
    cx, cy = chip // 4, chip % 4
    ha = jnp.where(core == 0, cy, cx)
    qb = jnp.where(core == 0, cx, cy)
    half = cx // 2
    mate = me + 1 - 2 * core

    def place(a, b):
        return jnp.where(core == 0, (b * 4 + a) * 2, (a * 4 + b) * 2 + 1)

    def remote(src, dst, k, r, device):
        return pltpu.make_async_remote_copy(
            src_ref=src, dst_ref=dst, send_sem=send_sems.at[k], recv_sem=recv_sems.at[r],
            device_id=device, device_id_type=MESH,
        )

    barrier = pltpu.get_barrier_semaphore()

    def greet(device):
        pl.semaphore_signal(barrier, inc=1, device_id=device, device_id_type=MESH)

    def at(px, py, pc):
        return {"seq": (px * 4 + py) * 2 + pc}

    greet({"seq": mate})
    for d in range(1, 4):
        greet({"dp": (night + d) % 4})
        for pc in range(2):
            greet(at((cx + d) % 4, cy, pc))
            greet(at(cx, (cy + d) % 4, pc))
    own_copy = pltpu.make_async_copy(samples_hbm, own, sems.at[6])
    own_copy.start()
    shard_copy = pltpu.make_async_copy(shard, shard_buf, sems.at[7])
    shard_copy.start()
    copies = [
        pltpu.make_async_copy(middle_hbm.at[l], middle.at[l], sems.at[l]) for l in range(4)
    ]
    copies.append(pltpu.make_async_copy(last_hbm, last, sems.at[4]))
    copies.append(pltpu.make_async_copy(proj_hbm, proj, sems.at[5]))
    for copy in copies:
        copy.start()

    is_odd = core
    group_len = length[0, 0]
    even_len = jnp.where(is_odd == 1, 2 * FR - group_len, group_len)
    n1 = jnp.where(is_odd == 1, jnp.maximum(even_len - FR, 0), jnp.minimum(even_len, FR))
    own_rows = own.shape[0]

    def source(r):
        even = jnp.where(r < even_len, r, own_rows + r - even_len)
        odd = jnp.where(
            r + FR < even_len, own_rows + r + FR - (own_rows - SWAP), r + FR - even_len
        )
        return jnp.where(is_odd == 1, odd, even)

    def picks(width, base, step):
        r = lax.broadcasted_iota(jnp.int32, (FR + TAIL, width), 0)
        col = lax.broadcasted_iota(jnp.int32, (FR + TAIL, width), 1) + base
        src = jnp.where(
            r < FR, source(r) + step, source(jnp.where(r == FR, n1 - 1, FR - 1)) + 1
        )
        return onehot(src == col)

    shard_copy.wait()
    gr = lax.broadcasted_iota(jnp.int32, (32, 20), 0)
    gc = lax.broadcasted_iota(jnp.int32, (32, 20), 1)
    zbuf[night] = dot(onehot(gr == gc), shard_buf[...]).astype(BF)
    own_copy.wait()
    sr = lax.broadcasted_iota(jnp.int32, (SWAP, own_rows), 0)
    sc = lax.broadcasted_iota(jnp.int32, (SWAP, own_rows), 1)
    pick_swap = onehot(sc == sr + jnp.where(core == 0, own_rows - SWAP, 0))
    for c in range(0, 2560, 512):
        outgoing[:, c : c + 512] = dot(pick_swap, own[:, c : c + 512]).astype(BF)
    pl.semaphore_wait(barrier, 16)
    swap = remote(outgoing, arr, 20, 20, {"seq": mate})
    swap.start()
    mine_z = zbuf.at[night]
    zcopies = [
        remote(mine_z, mine_z, 16 + d, 16 + (4 - d) % 4, {"dp": (night + d) % 4})
        for d in range(1, 4)
    ]
    for copy in zcopies:
        copy.start()
    pick_own = picks(own_rows, 0, 0)
    for c in range(0, 2560, 512):
        x[:, c : c + 512] = dot(pick_own, own[:, c : c + 512]).astype(BF)
    x[:, 2560:2688] = dot(picks(own_rows, 0, 1), own[:, :128]).astype(BF)
    mout[...] = jnp.zeros_like(mout)
    er = lax.broadcasted_iota(jnp.int32, (256, 80), 0)
    ec = lax.broadcasted_iota(jnp.int32, (256, 80), 1)

    def shift(u, carry):
        shifted[u] = dot(onehot(er == ec + lax.rem(40 * u, 128)), first[...]).astype(BF)
        return carry

    lax.fori_loop(0, 16, shift, 0)

    slot = me - 16 * half
    first_hops = []
    for d in range(4):
        ty, tx = (cy + d) % 4, (cx + d) % 4
        first_hops.append((
            at(cx, ty, half),
            remote(wblk.at[0], wbuf.at[0, slot], 48 + d, 48 + slot % 8, at(cx, ty, half)),
        ))
        first_hops.append((
            at(tx, cy, half),
            remote(
                wblk.at[1], wbuf.at[1, slot], 52 + d, 56 + (cx % 2) * 2 + core, at(tx, cy, half)
            ),
        ))
    def start_weights():
        for copy in zcopies:
            copy.wait_recv()
        cr = lax.broadcasted_iota(jnp.int32, (80, 128), 0)
        cc = lax.broadcasted_iota(jnp.int32, (80, 128), 1)
        packed = dot(
            onehot(cc == 32 * (cr // 20) + cr % 20), zbuf[...].reshape(128, zbuf.shape[2])
        ).astype(BF)
        wide = packed.shape[1] // 2
        wblk[0] = packed[:, :wide]
        wblk[1] = packed[:, wide:]
        for target, copy in first_hops:

            @pl.when(target["seq"] != me)
            def _():
                copy.start()

        @pl.when(half == core)
        def _():
            wbuf[0, slot] = wblk[0]
            wbuf[1, slot] = wblk[1]

    row_slots = pl.ds(8 * (cx % 2), 8)
    x_hops = [
        remote(
            wbuf.at[0, row_slots], wbuf.at[0, row_slots], 60 + d, 60 + cx % 2,
            at((cx + d) % 4, cy, core),
        )
        for d in (2, 1, 3)
    ]
    y_hops = [
        remote(
            wbuf.at[1, pl.ds(8 * p + 2 * cy, 2)], wbuf.at[1, pl.ds(8 * p + 2 * cy, 2)],
            64 + 2 * d + p, 64 + 2 * (4 - d) + p, at(cx, (cy + d) % 4, core),
        )
        for d in (2, 1, 3)
        for p in range(2)
    ]

    def second_hops():
        for k in range(8):

            @pl.when((half == core) & (k != slot % 8))
            def _():
                remote(
                    wblk.at[0], wbuf.at[0, 8 * (cx % 2) + k], 48, 48 + k, {"seq": mate}
                ).wait_recv()

        @pl.when(half == core)
        def _():
            for copy in x_hops:
                copy.start()

        for k in range(4):
            from_x, from_core = 2 * core + k // 2, k % 2

            @pl.when((from_x != cx) | (from_core != core))
            def _():
                remote(
                    wblk.at[1], wbuf.at[1, 8 * (k // 2) + 2 * cy + from_core], 52, 56 + k,
                    {"seq": mate},
                ).wait_recv()

        for copy in y_hops:
            copy.start()

    def weights_arrived():
        for p in range(2):

            @pl.when(2 * core + p != cx)
            def _():
                remote(
                    wbuf.at[0, pl.ds(8 * p, 8)], wbuf.at[0, pl.ds(8 * p, 8)], 60, 60 + p,
                    {"seq": mate},
                ).wait_recv()

        for d in range(1, 4):
            for p in range(2):
                block = wbuf.at[1, pl.ds(8 * p + 2 * ((cy + d) % 4), 2)]
                remote(block, block, 64, 64 + 2 * d + p, {"seq": mate}).wait_recv()

    def weights_sent():
        for target, copy in first_hops:

            @pl.when(target["seq"] != me)
            def _():
                copy.wait_send()

        @pl.when(half == core)
        def _():
            for copy in x_hops:
                copy.wait_send()

        for copy in y_hops:
            copy.wait_send()

    swap.wait_recv()
    pick_arr = picks(SWAP, own_rows, 0)
    for c in range(0, 2560, 512):
        x[:, c : c + 512] += dot(pick_arr, arr[:, c : c + 512]).astype(BF)
    x[:, 2560:2688] += dot(picks(SWAP, own_rows, 1), arr[:, :128]).astype(BF)

    nr = lax.broadcasted_iota(jnp.int32, (FR, FR + TAIL), 0)
    nc = lax.broadcasted_iota(jnp.int32, (FR, FR + TAIL), 1)
    following = jnp.where(nr == n1 - 1, FR, jnp.where(nr == FR - 1, FR + 1, nr + 1))
    pick_next = (following == nc).astype(F32).astype(BF)

    def close(a, t):
        body = jnp.concatenate([a[0, :, :CH], t[0, :, :CH]], axis=0)
        a[a.shape[0] - 1, :, :CH] = dot(pick_next, body).astype(BF)

    def layer_one(u, acc, parity, half):
        offset = lax.rem(40 * u, 128)
        base = pl.multiple_of(40 * u - offset, 128)
        parts = [x[:FR, pl.ds(pl.multiple_of(base + 640 * b, 128), 256)] for b in range(4)]
        parts.append(x[FR:, pl.ds(base, 256)])
        acc[...] = dot(jnp.concatenate(parts, axis=0), shifted[u])

        def out(r, n, val):
            if r < 4 * FR:
                a1[8 * (r // FR) + half, r % FR : r % FR + n, parity * CH : parity * CH + CH] = val
            else:
                t1[half, :, parity * CH : parity * CH + CH] = val

        settle(acc, 4 * FR + TAIL, 1e-5, out)

    def one_step(i, carry):
        for k, acc in enumerate((acc0, acc1, acc2, acc3)):
            layer_one(4 * i + k, acc, k % 2, 2 * i + k // 2)
        return carry

    lax.fori_loop(0, 1, one_step, 0)
    start_weights()
    lax.fori_loop(1, 4, one_step, 0)
    second_hops()
    close(a1, t1)

    def three_taps(ain, start, count, rows, layer, acc):
        pairs = ain[pl.ds(start, count)].reshape(count * rows, 2 * CH)
        ahead = ain[pl.ds(start + 1, count), :, :CH].reshape(count * rows, CH)
        acc[: count * rows, :] = dot(
            jnp.concatenate([pairs, ahead], axis=1), middle[layer]
        )

    def main_chunk(ain, aout, layer, i, acc):
        three_taps(ain, 4 * i, 4, FR, layer, acc)

        def out(r, n, val):
            s = r // FR
            aout[2 * i + s // 2, r % FR : r % FR + n, (s % 2) * CH : (s % 2) * CH + CH] = val

        settle(acc, 4 * FR, 2e-5, out)

    def tail_chunk(tin, tout, layer, count, acc):
        three_taps(tin, 0, count, TAIL, layer, acc)

        def out(r, n, val):
            for k in range(n // TAIL):
                s = (r + k * TAIL) // TAIL
                tout[s // 2, :, (s % 2) * CH : (s % 2) * CH + CH] = val[k * TAIL : (k + 1) * TAIL]

        settle(acc, count * TAIL, 2e-5, out)

    def layer(ain, aout, tin, tout, index, chunks, tail_count):
        copies[index].wait()

        def step(i, carry):
            for k, acc in enumerate((acc0, acc1, acc2, acc3)):
                main_chunk(ain, aout, index, 4 * i + k, acc)
            return carry

        if chunks >= 4:
            lax.fori_loop(0, chunks // 4, step, 0)
        else:
            for k in range(chunks):
                main_chunk(ain, aout, index, k, (acc0, acc1)[k])
        if tail_count:
            tail_chunk(tin, tout, index, tail_count, acc2)
            close(aout, tout)

    layer(a1, a2, t1, t2, 0, 8, 7)
    layer(a2, a3, t2, t3, 1, 4, 3)
    layer(a3, a4, t3, t4, 2, 2, 1)
    layer(a4, a5, None, None, 3, 1, 0)

    copies[4].wait()
    acc0[: 2 * FR, :] = dot(a5[...].reshape(2 * FR, 2 * CH), last[0])

    def out6(r, n, val):
        a6[r % FR : r % FR + n, (r // FR) * CH : (r // FR) * CH + CH] = val

    settle(acc0, 2 * FR, 2e-5, out6)
    acc1[:FR, :] = dot(a6[...], last[1])
    feats = []
    settle(acc1, FR, 2e-5, lambda r, n, val: feats.append(val))
    frame_feat = jnp.concatenate(feats, axis=0).astype(F32)
    normed_feat = (row_norm(frame_feat, 2e-5) * gain[...]).astype(BF)
    copies[5].wait()
    hidden = (dot(normed_feat, proj[...]) + bias[...]).astype(BF)
    hidden_buf[...] = hidden
    normed2[pl.ds(pl.multiple_of(core * FR, FR), FR), :] = (
        row_norm(hidden.astype(F32), 1e-5) * attn_gain[...]
    ).astype(BF)
    mine = normed2.at[pl.ds(pl.multiple_of(core * FR, FR), FR)]
    exchange = remote(mine, mine, 21, 21, {"seq": mate})
    exchange.start()
    weights_arrived()
    exchange.wait_recv()

    def head_weights(h):
        return jnp.concatenate(
            [wbuf[p, pl.ds(4 * h, 4)].reshape(320, wbuf.shape[3]) for p in range(2)], axis=1
        )

    yr = lax.broadcasted_iota(jnp.int32, (320, 1), 0)
    row_scale = jnp.where(yr % 80 < 20, SCALE, 1.0).astype(F32)
    pr = lax.broadcasted_iota(jnp.int32, (240, 320), 0)
    pc = lax.broadcasted_iota(jnp.int32, (240, 320), 1)
    regroup = onehot(pc == 80 * ((pr % 80) // 20) + 20 * (pr // 80) + pr % 20)

    def project(h, carry):
        y = lax.dot_general(head_weights(h), normed2[...], NT, preferred_element_type=F32)
        ysend[h] = dot(regroup, (y * row_scale).astype(BF)).astype(BF)
        return carry

    forwards = []

    def forward(d, block):
        for e in range(1, 4):
            copy = remote(
                block.at[pl.ds(80, 160)], kvbuf.at[qb, (ha + d) % 4],
                28 + 4 * d + e, 28 + 4 * d + (4 - e) % 4, {"seq": place(ha, (qb + e) % 4)},
            )
            copy.start()
            forwards.append(copy)

    heads = []
    for d in (0, 1, 3, 2):
        to = (ha + d) % 4
        project(to, 0)
        if d == 0:
            forward(0, ysend.at[ha])
            continue
        heads.append(
            remote(ysend.at[to], qkv.at[ha], 24 + d, 24 + (4 - d) % 4, {"seq": place(to, qb)})
        )
        heads[-1].start()
    qkv[ha] = ysend[ha]
    wr = lax.broadcasted_iota(jnp.int32, (128, 320), 0)
    wc = lax.broadcasted_iota(jnp.int32, (128, 320), 1)
    pick_out = onehot((wc == 80 * (wr // 20) + 60 + wr % 20) & (wr < 80))
    for h in range(4):
        out_weight[128 * h : 128 * h + 128, :] = dot(pick_out, head_weights(h)).astype(BF)
    for d in (3, 1, 2):
        remote(ysend.at[0], qkv.at[(ha + d) % 4], 24, 24 + d, {"seq": mate}).wait_recv()
        forward(d, qkv.at[(ha + d) % 4])

    for i in range(4):
        qs[i] = jnp.transpose(qkv[i, :80, :].astype(F32)).astype(BF)

    def masses(values):
        ones = jnp.ones((16, values.shape[1]), BF)
        return jnp.concatenate([values, ones], axis=0)

    def attend(keys, values, is_first, finish=None):
        def step(i, carry):
            for rows in (slice(0, 128), slice(128, 256)):
                s = dot(qs[i, rows], keys)
                top = jnp.max(s, axis=-1, keepdims=True)
                if not is_first:
                    top = jnp.maximum(top, peak[i, rows])
                p = jnp.exp2(s - top).astype(BF)
                o = lax.dot_general(p, masses(values), NT, preferred_element_type=F32)
                if not is_first:
                    o = o + accum[i, rows] * jnp.exp2(peak[i, rows] - top)
                peak[i, rows] = top
                accum[i, rows] = o
            return carry

        if finish is None:
            for i in range(4):
                step(i, 0)
        else:
            for d in (1, 2, 3, 0):
                step((ha + d) % 4, 0)
                finish(d)

    returns = []
    keep2 = pltpu.make_async_copy(mout.at[ha], mbuf.at[ha], sems.at[9])

    def give_back(d):
        to = (ha + d) % 4
        mout[to, :, :80] = (accum[to, :, :80] / accum[to, :, 80:81]).astype(BF)
        if d == 0:
            keep2.start()
        else:
            returns.append(
                remote(mout.at[to], mbuf.at[ha], 44 + d, 44 + (4 - d) % 4, {"seq": place(to, qb)})
            )
            returns[-1].start()

    for d in (0, 3, 1, 2):
        a = (ha + d) % 4
        for e in range(1, 4):
            remote(
                qkv.at[0, pl.ds(80, 160)], kvbuf.at[(qb + e) % 4, a], 28, 28 + 4 * d + e,
                {"seq": mate},
            ).wait_recv()
        blocks = [qkv[a, 80:, :]] + [kvbuf[(qb + e) % 4, a] for e in range(1, 4)]
        attend(
            jnp.concatenate([block[:80] for block in blocks], axis=1),
            jnp.concatenate([block[80:] for block in blocks], axis=1),
            d == 0,
            give_back if d == 2 else None,
        )
    keep2.wait()
    for d in range(1, 4):
        remote(mout.at[0], mbuf.at[(ha + d) % 4], 44, 44 + d, {"seq": mate}).wait_recv()

    def output(rows_of):
        rows = pl.ds(pl.multiple_of(rows_of * FR, FR), FR)
        mixed = jnp.concatenate([mbuf[h, rows, :] for h in range(4)], axis=1)
        return dot(mixed, out_weight[...])

    psend[...] = output(1 - core).astype(BF)
    last_swap = remote(psend, precv, 22, 22, {"seq": mate})
    last_swap.start()
    base = hidden_buf[...].astype(F32) + output(core)
    last_swap.wait_recv()
    out_ref[...] = (base + precv[...].astype(F32)).astype(BF)

    for copy in [swap, exchange, last_swap] + zcopies + heads + forwards + returns:
        copy.wait_send()
    weights_sent()


def call(length, samples, shard, first, middle, last, gain, proj, bias, attn_gain):
    vmem = pl.BlockSpec(memory_space=pltpu.VMEM)
    hbm = pl.BlockSpec(memory_space=pl.ANY)
    rows, block = samples.shape
    width = proj.shape[1]
    return pl.pallas_call(
        kernel,
        out_shape=jax.ShapeDtypeStruct((FR, width), BF),
        in_specs=[
            pl.BlockSpec(memory_space=pltpu.SMEM), hbm, hbm, vmem, hbm, hbm, vmem, hbm, vmem, vmem,
        ],
        out_specs=vmem,
        scratch_shapes=[
            pltpu.VMEM((rows, block), BF),
            pltpu.VMEM((SWAP, block), BF),
            pltpu.VMEM((SWAP, block), BF),
            pltpu.VMEM((FR + TAIL, block + 128), BF),
            pltpu.VMEM((33, FR, 2 * CH), BF),
            pltpu.VMEM((17, FR, 2 * CH), BF),
            pltpu.VMEM((9, FR, 2 * CH), BF),
            pltpu.VMEM((5, FR, 2 * CH), BF),
            pltpu.VMEM((2, FR, 2 * CH), BF),
            pltpu.VMEM((FR, 2 * CH), BF),
            pltpu.VMEM((8, TAIL, 2 * CH), BF),
            pltpu.VMEM((4, TAIL, 2 * CH), BF),
            pltpu.VMEM((2, TAIL, 2 * CH), BF),
            pltpu.VMEM((1, TAIL, 2 * CH), BF),
            pltpu.VMEM((4 * FR + TAIL, CH), F32),
            pltpu.VMEM((4 * FR + TAIL, CH), F32),
            pltpu.VMEM(middle.shape, BF),
            pltpu.VMEM(last.shape, BF),
            pltpu.VMEM(proj.shape, BF),
            pltpu.VMEM((16, 256, CH), BF),
            pltpu.VMEM((4 * FR + TAIL, CH), F32),
            pltpu.VMEM((4 * FR + TAIL, CH), F32),
            pltpu.VMEM((20, width), BF),
            pltpu.VMEM((4, 32, width), BF),
            pltpu.VMEM((2, 80, width // 2), BF),
            pltpu.VMEM((2, 16, 80, width // 2), BF),
            pltpu.VMEM((2 * FR, width), BF),
            pltpu.VMEM((FR, width), BF),
            pltpu.VMEM((4, 240, 256), BF),
            pltpu.VMEM((4, 240, 256), BF),
            pltpu.VMEM((4, 4, 160, 256), BF),
            pltpu.VMEM((4, 256, 80), BF),
            pltpu.VMEM((4, 256, 1), F32),
            pltpu.VMEM((4, 256, 96), F32),
            pltpu.VMEM((4, 256, 128), BF),
            pltpu.VMEM((4, 256, 128), BF),
            pltpu.VMEM((512, width), BF),
            pltpu.VMEM((FR, width), BF),
            pltpu.VMEM((FR, width), BF),
            pltpu.SemaphoreType.DMA((10,)),
            pltpu.SemaphoreType.DMA((72,)),
            pltpu.SemaphoreType.DMA((72,)),
        ],
        compiler_params=pltpu.CompilerParams(
            vmem_limit_bytes=60 << 20, collective_id=0, has_side_effects=True
        ),
        cost_estimate=pl.CostEstimate(
            flops=20 * 10**9, bytes_accessed=20 * 10**6, transcendentals=13 * 10**6
        ),
        name="encoder",
    )(
        length, samples, shard, first, middle, last, gain, proj, bias,
        attn_gain,
    )


def body(
    group_samples, group_lengths, group_offsets, conv_first, conv_middle, conv_last,
    feat_gain, proj_weight, proj_bias, attn_gain, attn_weight,
):
    encoded = call(
        group_lengths, group_samples[0, 0], attn_weight.T, conv_first, conv_middle, conv_last,
        feat_gain, proj_weight, proj_bias, attn_gain,
    )
    return encoded.reshape(1, FR, -1)


def solution(mesh):
    in_specs = (
        P("dp", "seq", None, None), P("dp", "seq"), P("dp", "seq"),
        P(), P(), P(), P(), P(), P(), P(), P(None, ("dp", "seq")),
    )
    out_specs = P("dp", "seq", None)
    return jax.shard_map(body, mesh=mesh, in_specs=in_specs, out_specs=out_specs, check_vma=False)
```

```python
import math

import jax
import jax.numpy as jnp
from jax import lax
from jax.experimental import pallas as pl
from jax.experimental.pallas import tpu as pltpu
from jax.sharding import PartitionSpec as P

FR = 128
CH = 512
TAIL = 16
SWAP = 80
BF = jnp.bfloat16
F32 = jnp.float32
SCALE = math.log2(math.e) / math.sqrt(80)


def dot(a, b):
    return jnp.dot(a, b, preferred_element_type=F32)


def row_norm(v, eps):
    center = jnp.mean(v, axis=-1, keepdims=True)
    d = v - center
    spread = jnp.mean(d * d, axis=-1, keepdims=True)
    return d * lax.rsqrt(spread + eps)


def settle(acc, rows, eps, out):
    for r in range(0, rows, 64):
        n = min(64, rows - r)
        v = acc[r : r + n, :]
        center = jnp.mean(v, axis=-1, keepdims=True)
        d = v - center
        spread = jnp.mean(d * d, axis=-1, keepdims=True)
        u = d * lax.rsqrt(2.0 * spread + 2.0 * eps)
        out(r, n, (u + u * lax.erf(u)).astype(BF))


MESH = pl.DeviceIdType.MESH
NT = (((1,), (1,)), ((), ()))


def onehot(mask):
    return mask.astype(F32).astype(BF)


def kernel(
    length, samples_hbm, shard, first, middle_hbm, last_hbm, gain, proj_hbm, bias, attn_gain,
    out_ref,
    own, outgoing, arr, x, a1, a2, a3, a4, a5, a6, t1, t2, t3, t4, acc0, acc1, middle, last, proj,
    shifted, acc2, acc3, shard_buf, zbuf, wblk, wbuf, normed2, hidden_buf, ysend, qkv, kvbuf, qs, peak, accum,
    mout, mbuf, out_weight, psend, precv, sems, send_sems, recv_sems,
):
    me = lax.axis_index("seq")
    night = lax.axis_index("dp")
    core = me % 2
    chip = me // 2
    cx, cy = chip // 4, chip % 4
    ha = jnp.where(core == 0, cy, cx)
    qb = jnp.where(core == 0, cx, cy)
    half = cx // 2
    mate = me + 1 - 2 * core

    def place(a, b):
        return jnp.where(core == 0, (b * 4 + a) * 2, (a * 4 + b) * 2 + 1)

    def remote(src, dst, k, r, device):
        return pltpu.make_async_remote_copy(
            src_ref=src, dst_ref=dst, send_sem=send_sems.at[k], recv_sem=recv_sems.at[r],
            device_id=device, device_id_type=MESH,
        )

    barrier = pltpu.get_barrier_semaphore()

    def greet(device):
        pl.semaphore_signal(barrier, inc=1, device_id=device, device_id_type=MESH)

    def at(px, py, pc):
        return {"seq": (px * 4 + py) * 2 + pc}

    greet({"seq": mate})
    for d in range(1, 4):
        greet({"dp": (night + d) % 4})
        for pc in range(2):
            greet(at((cx + d) % 4, cy, pc))
            greet(at(cx, (cy + d) % 4, pc))
    own_copy = pltpu.make_async_copy(samples_hbm, own, sems.at[6])
    own_copy.start()
    shard_copy = pltpu.make_async_copy(shard, shard_buf, sems.at[7])
    shard_copy.start()
    copies = [
        pltpu.make_async_copy(middle_hbm.at[l], middle.at[l], sems.at[l]) for l in range(4)
    ]
    copies.append(pltpu.make_async_copy(last_hbm, last, sems.at[4]))
    copies.append(pltpu.make_async_copy(proj_hbm, proj, sems.at[5]))
    for copy in copies:
        copy.start()

    is_odd = core
    group_len = length[0, 0]
    even_len = jnp.where(is_odd == 1, 2 * FR - group_len, group_len)
    n1 = jnp.where(is_odd == 1, jnp.maximum(even_len - FR, 0), jnp.minimum(even_len, FR))
    own_rows = own.shape[0]

    def source(r):
        even = jnp.where(r < even_len, r, own_rows + r - even_len)
        odd = jnp.where(
            r + FR < even_len, own_rows + r + FR - (own_rows - SWAP), r + FR - even_len
        )
        return jnp.where(is_odd == 1, odd, even)

    def picks(width, base, step):
        r = lax.broadcasted_iota(jnp.int32, (FR + TAIL, width), 0)
        col = lax.broadcasted_iota(jnp.int32, (FR + TAIL, width), 1) + base
        src = jnp.where(
            r < FR, source(r) + step, source(jnp.where(r == FR, n1 - 1, FR - 1)) + 1
        )
        return onehot(src == col)

    shard_copy.wait()
    gr = lax.broadcasted_iota(jnp.int32, (32, 20), 0)
    gc = lax.broadcasted_iota(jnp.int32, (32, 20), 1)
    zbuf[night] = dot(onehot(gr == gc), shard_buf[...]).astype(BF)
    own_copy.wait()
    sr = lax.broadcasted_iota(jnp.int32, (SWAP, own_rows), 0)
    sc = lax.broadcasted_iota(jnp.int32, (SWAP, own_rows), 1)
    pick_swap = onehot(sc == sr + jnp.where(core == 0, own_rows - SWAP, 0))
    for c in range(0, 2560, 512):
        outgoing[:, c : c + 512] = dot(pick_swap, own[:, c : c + 512]).astype(BF)
    pl.semaphore_wait(barrier, 16)
    swap = remote(outgoing, arr, 20, 20, {"seq": mate})
    swap.start()
    mine_z = zbuf.at[night]
    zcopies = [
        remote(mine_z, mine_z, 16 + d, 16 + (4 - d) % 4, {"dp": (night + d) % 4})
        for d in range(1, 4)
    ]
    for copy in zcopies:
        copy.start()
    pick_own = picks(own_rows, 0, 0)
    for c in range(0, 2560, 512):
        x[:, c : c + 512] = dot(pick_own, own[:, c : c + 512]).astype(BF)
    x[:, 2560:2688] = dot(picks(own_rows, 0, 1), own[:, :128]).astype(BF)
    mout[...] = jnp.zeros_like(mout)
    er = lax.broadcasted_iota(jnp.int32, (256, 80), 0)
    ec = lax.broadcasted_iota(jnp.int32, (256, 80), 1)

    def shift(u, carry):
        shifted[u] = dot(onehot(er == ec + lax.rem(40 * u, 128)), first[...]).astype(BF)
        return carry

    lax.fori_loop(0, 16, shift, 0)

    slot = me - 16 * half
    first_hops = []
    for d in range(4):
        ty, tx = (cy + d) % 4, (cx + d) % 4
        first_hops.append((
            at(cx, ty, half),
            remote(wblk.at[0], wbuf.at[0, slot], 48 + d, 48 + slot % 8, at(cx, ty, half)),
        ))
        first_hops.append((
            at(tx, cy, half),
            remote(
                wblk.at[1], wbuf.at[1, slot], 52 + d, 56 + (cx % 2) * 2 + core, at(tx, cy, half)
            ),
        ))
    def start_weights():
        for copy in zcopies:
            copy.wait_recv()
        cr = lax.broadcasted_iota(jnp.int32, (80, 128), 0)
        cc = lax.broadcasted_iota(jnp.int32, (80, 128), 1)
        packed = dot(
            onehot(cc == 32 * (cr // 20) + cr % 20), zbuf[...].reshape(128, zbuf.shape[2])
        ).astype(BF)
        wide = packed.shape[1] // 2
        wblk[0] = packed[:, :wide]
        wblk[1] = packed[:, wide:]
        for target, copy in first_hops:

            @pl.when(target["seq"] != me)
            def _():
                copy.start()

        @pl.when(half == core)
        def _():
            wbuf[0, slot] = wblk[0]
            wbuf[1, slot] = wblk[1]

    row_slots = pl.ds(8 * (cx % 2), 8)
    x_hops = [
        remote(
            wbuf.at[0, row_slots], wbuf.at[0, row_slots], 60 + d, 60 + cx % 2,
            at((cx + d) % 4, cy, core),
        )
        for d in (2, 1, 3)
    ]
    y_hops = [
        remote(
            wbuf.at[1, pl.ds(8 * p + 2 * cy, 2)], wbuf.at[1, pl.ds(8 * p + 2 * cy, 2)],
            64 + 2 * d + p, 64 + 2 * (4 - d) + p, at(cx, (cy + d) % 4, core),
        )
        for d in (2, 1, 3)
        for p in range(2)
    ]

    def second_hops():
        for k in range(8):

            @pl.when((half == core) & (k != slot % 8))
            def _():
                remote(
                    wblk.at[0], wbuf.at[0, 8 * (cx % 2) + k], 48, 48 + k, {"seq": mate}
                ).wait_recv()

        @pl.when(half == core)
        def _():
            for copy in x_hops:
                copy.start()

        for k in range(4):
            from_x, from_core = 2 * core + k // 2, k % 2

            @pl.when((from_x != cx) | (from_core != core))
            def _():
                remote(
                    wblk.at[1], wbuf.at[1, 8 * (k // 2) + 2 * cy + from_core], 52, 56 + k,
                    {"seq": mate},
                ).wait_recv()

        for copy in y_hops:
            copy.start()

    def weights_arrived():
        for p in range(2):

            @pl.when(2 * core + p != cx)
            def _():
                remote(
                    wbuf.at[0, pl.ds(8 * p, 8)], wbuf.at[0, pl.ds(8 * p, 8)], 60, 60 + p,
                    {"seq": mate},
                ).wait_recv()

        for d in range(1, 4):
            for p in range(2):
                block = wbuf.at[1, pl.ds(8 * p + 2 * ((cy + d) % 4), 2)]
                remote(block, block, 64, 64 + 2 * d + p, {"seq": mate}).wait_recv()

    def weights_sent():
        for target, copy in first_hops:

            @pl.when(target["seq"] != me)
            def _():
                copy.wait_send()

        @pl.when(half == core)
        def _():
            for copy in x_hops:
                copy.wait_send()

        for copy in y_hops:
            copy.wait_send()

    swap.wait_recv()
    pick_arr = picks(SWAP, own_rows, 0)
    for c in range(0, 2560, 512):
        x[:, c : c + 512] += dot(pick_arr, arr[:, c : c + 512]).astype(BF)
    x[:, 2560:2688] += dot(picks(SWAP, own_rows, 1), arr[:, :128]).astype(BF)

    nr = lax.broadcasted_iota(jnp.int32, (FR, FR + TAIL), 0)
    nc = lax.broadcasted_iota(jnp.int32, (FR, FR + TAIL), 1)
    following = jnp.where(nr == n1 - 1, FR, jnp.where(nr == FR - 1, FR + 1, nr + 1))
    pick_next = (following == nc).astype(F32).astype(BF)

    def close(a, t):
        body = jnp.concatenate([a[0, :, :CH], t[0, :, :CH]], axis=0)
        a[a.shape[0] - 1, :, :CH] = dot(pick_next, body).astype(BF)

    def layer_one(u, acc, parity, half):
        offset = lax.rem(40 * u, 128)
        base = pl.multiple_of(40 * u - offset, 128)
        parts = [x[:FR, pl.ds(pl.multiple_of(base + 640 * b, 128), 256)] for b in range(4)]
        parts.append(x[FR:, pl.ds(base, 256)])
        acc[...] = dot(jnp.concatenate(parts, axis=0), shifted[u])

        def out(r, n, val):
            if r < 4 * FR:
                a1[8 * (r // FR) + half, r % FR : r % FR + n, parity * CH : parity * CH + CH] = val
            else:
                t1[half, :, parity * CH : parity * CH + CH] = val

        settle(acc, 4 * FR + TAIL, 1e-5, out)

    def one_step(i, carry):
        for k, acc in enumerate((acc0, acc1, acc2, acc3)):
            layer_one(4 * i + k, acc, k % 2, 2 * i + k // 2)
        return carry

    lax.fori_loop(0, 1, one_step, 0)
    start_weights()
    lax.fori_loop(1, 4, one_step, 0)
    second_hops()
    close(a1, t1)

    def three_taps(ain, start, count, rows, layer, acc):
        pairs = ain[pl.ds(start, count)].reshape(count * rows, 2 * CH)
        ahead = ain[pl.ds(start + 1, count), :, :CH].reshape(count * rows, CH)
        acc[: count * rows, :] = dot(
            jnp.concatenate([pairs, ahead], axis=1), middle[layer]
        )

    def main_chunk(ain, aout, layer, i, acc):
        three_taps(ain, 4 * i, 4, FR, layer, acc)

        def out(r, n, val):
            s = r // FR
            aout[2 * i + s // 2, r % FR : r % FR + n, (s % 2) * CH : (s % 2) * CH + CH] = val

        settle(acc, 4 * FR, 2e-5, out)

    def tail_chunk(tin, tout, layer, count, acc):
        three_taps(tin, 0, count, TAIL, layer, acc)

        def out(r, n, val):
            for k in range(n // TAIL):
                s = (r + k * TAIL) // TAIL
                tout[s // 2, :, (s % 2) * CH : (s % 2) * CH + CH] = val[k * TAIL : (k + 1) * TAIL]

        settle(acc, count * TAIL, 2e-5, out)

    def layer(ain, aout, tin, tout, index, chunks, tail_count):
        copies[index].wait()

        def step(i, carry):
            for k, acc in enumerate((acc0, acc1, acc2, acc3)):
                main_chunk(ain, aout, index, 4 * i + k, acc)
            return carry

        if chunks >= 4:
            lax.fori_loop(0, chunks // 4, step, 0)
        else:
            for k in range(chunks):
                main_chunk(ain, aout, index, k, (acc0, acc1)[k])
        if tail_count:
            tail_chunk(tin, tout, index, tail_count, acc2)
            close(aout, tout)

    layer(a1, a2, t1, t2, 0, 8, 7)
    layer(a2, a3, t2, t3, 1, 4, 3)
    layer(a3, a4, t3, t4, 2, 2, 1)
    layer(a4, a5, None, None, 3, 1, 0)

    copies[4].wait()
    acc0[: 2 * FR, :] = dot(a5[...].reshape(2 * FR, 2 * CH), last[0])

    def out6(r, n, val):
        a6[r % FR : r % FR + n, (r // FR) * CH : (r // FR) * CH + CH] = val

    settle(acc0, 2 * FR, 2e-5, out6)
    acc1[:FR, :] = dot(a6[...], last[1])
    feats = []
    settle(acc1, FR, 2e-5, lambda r, n, val: feats.append(val))
    frame_feat = jnp.concatenate(feats, axis=0).astype(F32)
    normed_feat = (row_norm(frame_feat, 2e-5) * gain[...]).astype(BF)
    copies[5].wait()
    hidden = (dot(normed_feat, proj[...]) + bias[...]).astype(BF)
    hidden_buf[...] = hidden
    normed2[pl.ds(pl.multiple_of(core * FR, FR), FR), :] = (
        row_norm(hidden.astype(F32), 1e-5) * attn_gain[...]
    ).astype(BF)
    mine = normed2.at[pl.ds(pl.multiple_of(core * FR, FR), FR)]
    exchange = remote(mine, mine, 21, 21, {"seq": mate})
    exchange.start()
    weights_arrived()
    exchange.wait_recv()

    def head_weights(h):
        return jnp.concatenate(
            [wbuf[p, pl.ds(4 * h, 4)].reshape(320, wbuf.shape[3]) for p in range(2)], axis=1
        )

    yr = lax.broadcasted_iota(jnp.int32, (320, 1), 0)
    row_scale = jnp.where(yr % 80 < 20, SCALE, 1.0).astype(F32)
    pr = lax.broadcasted_iota(jnp.int32, (240, 320), 0)
    pc = lax.broadcasted_iota(jnp.int32, (240, 320), 1)
    regroup = onehot(pc == 80 * ((pr % 80) // 20) + 20 * (pr // 80) + pr % 20)

    def project(h, carry):
        y = lax.dot_general(head_weights(h), normed2[...], NT, preferred_element_type=F32)
        ysend[h] = dot(regroup, (y * row_scale).astype(BF)).astype(BF)
        return carry

    forwards = []

    def forward(d, block):
        for e in range(1, 4):
            copy = remote(
                block.at[pl.ds(80, 160)], kvbuf.at[qb, (ha + d) % 4],
                28 + 4 * d + e, 28 + 4 * d + (4 - e) % 4, {"seq": place(ha, (qb + e) % 4)},
            )
            copy.start()
            forwards.append(copy)

    heads = []
    for d in (0, 2, 1, 3):
        to = (ha + d) % 4
        project(to, 0)
        if d == 0:
            forward(0, ysend.at[ha])
            continue
        heads.append(
            remote(ysend.at[to], qkv.at[ha], 24 + d, 24 + (4 - d) % 4, {"seq": place(to, qb)})
        )
        heads[-1].start()
    qkv[ha] = ysend[ha]
    wr = lax.broadcasted_iota(jnp.int32, (128, 320), 0)
    wc = lax.broadcasted_iota(jnp.int32, (128, 320), 1)
    pick_out = onehot((wc == 80 * (wr // 20) + 60 + wr % 20) & (wr < 80))
    for h in range(4):
        out_weight[128 * h : 128 * h + 128, :] = dot(pick_out, head_weights(h)).astype(BF)
    for d in (3, 1, 2):
        remote(ysend.at[0], qkv.at[(ha + d) % 4], 24, 24 + d, {"seq": mate}).wait_recv()
        forward(d, qkv.at[(ha + d) % 4])

    for i in range(4):
        qs[i] = jnp.transpose(qkv[i, :80, :].astype(F32)).astype(BF)

    def masses(values):
        ones = jnp.ones((16, values.shape[1]), BF)
        return jnp.concatenate([values, ones], axis=0)

    def attend(keys, values, is_first, finish=None):
        def step(i, carry):
            for rows in (slice(0, 128), slice(128, 256)):
                s = dot(qs[i, rows], keys)
                top = jnp.max(s, axis=-1, keepdims=True)
                if not is_first:
                    top = jnp.maximum(top, peak[i, rows])
                p = jnp.exp2(s - top).astype(BF)
                o = lax.dot_general(p, masses(values), NT, preferred_element_type=F32)
                if not is_first:
                    o = o + accum[i, rows] * jnp.exp2(peak[i, rows] - top)
                peak[i, rows] = top
                accum[i, rows] = o
            return carry

        if finish is None:
            for i in range(4):
                step(i, 0)
        else:
            for d in (1, 2, 3, 0):
                step((ha + d) % 4, 0)
                finish(d)

    returns = []
    keep2 = pltpu.make_async_copy(mout.at[ha], mbuf.at[ha], sems.at[9])

    def give_back(d):
        to = (ha + d) % 4
        mout[to, :, :80] = (accum[to, :, :80] / accum[to, :, 80:81]).astype(BF)
        if d == 0:
            keep2.start()
        else:
            returns.append(
                remote(mout.at[to], mbuf.at[ha], 44 + d, 44 + (4 - d) % 4, {"seq": place(to, qb)})
            )
            returns[-1].start()

    for d in (0, 3, 1, 2):
        a = (ha + d) % 4
        for e in range(1, 4):
            remote(
                qkv.at[0, pl.ds(80, 160)], kvbuf.at[(qb + e) % 4, a], 28, 28 + 4 * d + e,
                {"seq": mate},
            ).wait_recv()
        blocks = [qkv[a, 80:, :]] + [kvbuf[(qb + e) % 4, a] for e in range(1, 4)]
        attend(
            jnp.concatenate([block[:80] for block in blocks], axis=1),
            jnp.concatenate([block[80:] for block in blocks], axis=1),
            d == 0,
            give_back if d == 2 else None,
        )
    keep2.wait()
    for d in range(1, 4):
        remote(mout.at[0], mbuf.at[(ha + d) % 4], 44, 44 + d, {"seq": mate}).wait_recv()

    def output(rows_of):
        rows = pl.ds(pl.multiple_of(rows_of * FR, FR), FR)
        mixed = jnp.concatenate([mbuf[h, rows, :] for h in range(4)], axis=1)
        return dot(mixed, out_weight[...])

    psend[...] = output(1 - core).astype(BF)
    last_swap = remote(psend, precv, 22, 22, {"seq": mate})
    last_swap.start()
    base = hidden_buf[...].astype(F32) + output(core)
    last_swap.wait_recv()
    out_ref[...] = (base + precv[...].astype(F32)).astype(BF)

    for copy in [swap, exchange, last_swap] + zcopies + heads + forwards + returns:
        copy.wait_send()
    weights_sent()


def call(length, samples, shard, first, middle, last, gain, proj, bias, attn_gain):
    vmem = pl.BlockSpec(memory_space=pltpu.VMEM)
    hbm = pl.BlockSpec(memory_space=pl.ANY)
    rows, block = samples.shape
    width = proj.shape[1]
    return pl.pallas_call(
        kernel,
        out_shape=jax.ShapeDtypeStruct((FR, width), BF),
        in_specs=[
            pl.BlockSpec(memory_space=pltpu.SMEM), hbm, hbm, vmem, hbm, hbm, vmem, hbm, vmem, vmem,
        ],
        out_specs=vmem,
        scratch_shapes=[
            pltpu.VMEM((rows, block), BF),
            pltpu.VMEM((SWAP, block), BF),
            pltpu.VMEM((SWAP, block), BF),
            pltpu.VMEM((FR + TAIL, block + 128), BF),
            pltpu.VMEM((33, FR, 2 * CH), BF),
            pltpu.VMEM((17, FR, 2 * CH), BF),
            pltpu.VMEM((9, FR, 2 * CH), BF),
            pltpu.VMEM((5, FR, 2 * CH), BF),
            pltpu.VMEM((2, FR, 2 * CH), BF),
            pltpu.VMEM((FR, 2 * CH), BF),
            pltpu.VMEM((8, TAIL, 2 * CH), BF),
            pltpu.VMEM((4, TAIL, 2 * CH), BF),
            pltpu.VMEM((2, TAIL, 2 * CH), BF),
            pltpu.VMEM((1, TAIL, 2 * CH), BF),
            pltpu.VMEM((4 * FR + TAIL, CH), F32),
            pltpu.VMEM((4 * FR + TAIL, CH), F32),
            pltpu.VMEM(middle.shape, BF),
            pltpu.VMEM(last.shape, BF),
            pltpu.VMEM(proj.shape, BF),
            pltpu.VMEM((16, 256, CH), BF),
            pltpu.VMEM((4 * FR + TAIL, CH), F32),
            pltpu.VMEM((4 * FR + TAIL, CH), F32),
            pltpu.VMEM((20, width), BF),
            pltpu.VMEM((4, 32, width), BF),
            pltpu.VMEM((2, 80, width // 2), BF),
            pltpu.VMEM((2, 16, 80, width // 2), BF),
            pltpu.VMEM((2 * FR, width), BF),
            pltpu.VMEM((FR, width), BF),
            pltpu.VMEM((4, 240, 256), BF),
            pltpu.VMEM((4, 240, 256), BF),
            pltpu.VMEM((4, 4, 160, 256), BF),
            pltpu.VMEM((4, 256, 80), BF),
            pltpu.VMEM((4, 256, 1), F32),
            pltpu.VMEM((4, 256, 96), F32),
            pltpu.VMEM((4, 256, 128), BF),
            pltpu.VMEM((4, 256, 128), BF),
            pltpu.VMEM((512, width), BF),
            pltpu.VMEM((FR, width), BF),
            pltpu.VMEM((FR, width), BF),
            pltpu.SemaphoreType.DMA((10,)),
            pltpu.SemaphoreType.DMA((72,)),
            pltpu.SemaphoreType.DMA((72,)),
        ],
        compiler_params=pltpu.CompilerParams(
            vmem_limit_bytes=60 << 20, collective_id=0, has_side_effects=True
        ),
        cost_estimate=pl.CostEstimate(
            flops=20 * 10**9, bytes_accessed=20 * 10**6, transcendentals=13 * 10**6
        ),
        name="encoder",
    )(
        length, samples, shard, first, middle, last, gain, proj, bias,
        attn_gain,
    )


def body(
    group_samples, group_lengths, group_offsets, conv_first, conv_middle, conv_last,
    feat_gain, proj_weight, proj_bias, attn_gain, attn_weight,
):
    encoded = call(
        group_lengths, group_samples[0, 0], attn_weight.T, conv_first, conv_middle, conv_last,
        feat_gain, proj_weight, proj_bias, attn_gain,
    )
    return encoded.reshape(1, FR, -1)


def solution(mesh):
    in_specs = (
        P("dp", "seq", None, None), P("dp", "seq"), P("dp", "seq"),
        P(), P(), P(), P(), P(), P(), P(), P(None, ("dp", "seq")),
    )
    out_specs = P("dp", "seq", None)
    return jax.shard_map(body, mesh=mesh, in_specs=in_specs, out_specs=out_specs, check_vma=False)
```
